128 devices in a mesh: row: 8 (over z, core), col: 16 (over x, y).
Axes of the slice: x: 4, y: 4, z: 4, core: 2. Of those that a mesh axis runs over, the one named last changes fastest.
Arguments:
- factor_panel: bfloat16 [4096, 31, 16, 256], P('row', None, 'col'), may hold values from -0.015625 to 0.015625
- solved_prev: bfloat16 [31, 16, 256, 512], P(None, 'col'), may hold values from -6 to 6
- rhs_last: float32 [4096, 512], P('row', 'col'), may hold values from -6 to 6
- inv_last: bfloat16 [4096, 4096], P('row'), may hold values from -1 to 3, as said below
- inv_prev: bfloat16 [1, 16, 256, 4096], P(None, 'col'), may hold values from -1 to 3, as said below
Outputs:
- updated_rhs: float32 [512, 31, 16, 256], P('row', None, 'col')
- solution_last: float32 [4096, 512], P('row', 'col')
- solution_prev: float32 [4096, 512], P('col', 'row')
The draws below stay inside these ranges and needn't reach their ends.
Inputs may be any that keep to these rules, and one draw needn't show every extreme that they name: `inv_last`: lower triangular with a positive diagonal. `inv_prev`: as a 4096 x 4096 matrix, lower triangular with a positive diagonal.
All inputs are finite; a program needn't handle non-finite values.
Results may differ from the reference program's by a relative error of at most 0.0055.
Values may be sent and summed in bfloat16 or wider, within the bound.
A program may use at most 128 MiB of HBM per device.

```python
import math
import jax
import jax.numpy as jnp
from jax import lax

B = 4096
C = 256
ROUNDS = 31
R = 512
RB = 1
PRE = 126976
N_COL = 16


def triangular_inverse(key, diag_low, diag_high):
    diag_key, below_key = jax.random.split(key)
    row_ids = lax.broadcasted_iota(jnp.int32, (B, B), 0)
    col_ids = lax.broadcasted_iota(jnp.int32, (B, B), 1)
    below_part = jax.random.normal(below_key, (B, B), jnp.float32) * (0.8 / math.sqrt(B))
    below_part = jnp.clip(below_part, -0.9, 0.9)
    diagonal_values = jax.random.uniform(diag_key, (B, 1), jnp.float32, diag_low, diag_high)
    return jnp.where(row_ids > col_ids, below_part, 0.0) + jnp.where(row_ids == col_ids, diagonal_values, 0.0)


def draw_inv_last(key, part):
    key = jax.random.fold_in(key, 1)
    matrix = triangular_inverse(key, 0.6, 1.6)
    return matrix.astype(jnp.bfloat16)


def draw_inv_prev(key, part):
    key = jax.random.fold_in(key, 2)
    matrix = triangular_inverse(key, 0.6, 1.6)
    return matrix.reshape(RB, N_COL, C, B).astype(jnp.bfloat16)


def block_levels(stream_key, dims, cuts, least, largest):
    gain, own = 1.0, jax.random.fold_in(stream_key, 6)
    for axis_at, blocks in cuts:
        heights = jnp.exp(jax.random.uniform(jax.random.fold_in(own, axis_at), (blocks,), jnp.float32, least / len(cuts), largest / len(cuts)))
        gain = gain * jnp.repeat(heights, dims[axis_at] // blocks).reshape([-1 if axis == axis_at else 1 for axis in range(len(dims))])
    return gain


def gaussian(rng, shape, width, most, cuts=(), kind=jnp.bfloat16):
    result = jax.random.normal(rng, shape, jnp.float32) * width
    if len(cuts) > 0:
        result = block_levels(rng, shape, cuts, -0.22, 0.18) * result
    return jnp.clip(result, min=-most, max=most).astype(kind)


def setup_inputs(seed: int = 0) -> dict:
    key_of = jax.random.split(jax.random.key(seed), 6)
    factor_panel = gaussian(key_of[0], (B, ROUNDS, N_COL, C), PRE ** -0.5, 0.015625, ((0, 8), (2, 16)))
    solved_prev = gaussian(key_of[1], (ROUNDS, N_COL, C, R), 1.0, 6.0, ((1, 16),))
    rhs_last = gaussian(key_of[2], (B, R), 1.0, 6.0, ((0, 8), (1, 16)), jnp.float32)
    inv_last = draw_inv_last(jax.random.fold_in(key_of[5], 71), 0)
    inv_prev = draw_inv_prev(jax.random.fold_in(key_of[5], 71), 0)
    return dict(factor_panel=factor_panel, solved_prev=solved_prev, rhs_last=rhs_last, inv_last=inv_last, inv_prev=inv_prev)


def reference(factor_panel, solved_prev, rhs_last, inv_last, inv_prev):
    block_cols = N_COL * C
    panel_three = factor_panel.reshape(B, ROUNDS, block_cols)
    known_three = solved_prev.reshape(ROUNDS, block_cols, R)

    def forward_round(running_sum, round_id):
        columns_cut = lax.dynamic_index_in_dim(panel_three, round_id, 1, keepdims=False)
        rows_cut = lax.dynamic_index_in_dim(known_three, round_id, 0, keepdims=False)
        product = jnp.dot(columns_cut.astype(jnp.float32), rows_cut.astype(jnp.float32), precision=lax.Precision.HIGHEST)
        return running_sum + product, None

    inner, _ = lax.scan(forward_round, jnp.zeros((B, R), jnp.float32), jnp.arange(ROUNDS, dtype=jnp.int32))
    residue = (rhs_last - inner).astype(jnp.bfloat16)
    forward_last = jnp.dot(inv_last, residue, preferred_element_type=jnp.float32).astype(jnp.bfloat16)
    solution_last = jnp.dot(inv_last.T, forward_last, preferred_element_type=jnp.float32)
    solution_half = solution_last.astype(jnp.bfloat16).astype(jnp.float32)

    def backward_round(round_id):
        columns_cut = lax.dynamic_index_in_dim(panel_three, round_id, 1, keepdims=False)
        rows_cut = lax.dynamic_index_in_dim(known_three, round_id, 0, keepdims=False)
        product = jnp.dot(columns_cut.astype(jnp.float32).T, solution_half, precision=lax.Precision.HIGHEST)
        return rows_cut.astype(jnp.float32) - product

    updated = lax.map(backward_round, jnp.arange(ROUNDS, dtype=jnp.int32)).reshape(PRE, R)
    updated_rhs = updated.T.reshape(R, ROUNDS, N_COL, C)
    prior_block = updated[PRE - B:].astype(jnp.bfloat16)
    solution_prev = jnp.dot(inv_prev.reshape(B, B).T, prior_block, preferred_element_type=jnp.float32)
    return updated_rhs, solution_last, solution_prev
```

```python
import functools

import jax
import jax.numpy as jnp
from jax import lax
from jax.experimental import pallas as pl
from jax.experimental.pallas import tpu as pltpu
from jax.sharding import PartitionSpec as P

ROWS = 8
COLS = 16
RING = 4
ROUNDS = 31
SIDES = 512
SHARE = 512
BLOCK = 256
WIDE = 32
OWN = 64
LAG_ADD = 4
LAG_END = 8
SLOTS = LAG_END + 1
F32 = jnp.float32
BF16 = jnp.bfloat16


def remote(src, dst, send_sem, recv_sem, row, col):
    return pltpu.make_async_remote_copy(
        src_ref=src,
        dst_ref=dst,
        send_sem=send_sem,
        recv_sem=recv_sem,
        device_id=(row, col),
        device_id_type=pl.DeviceIdType.MESH,
    )


def each(start, stop, body):
    def step(index, carry):
        body(index)
        return carry

    lax.fori_loop(start, stop, step, 0)


def kernel(
    panel_hbm, known_hbm, rhs_hbm, inv_hbm, prev_hbm,
    upd_hbm, last_hbm, sol_prev_hbm,
    panel, known, rhs, inv, prev,
    acc, send_b, recv_b, part_c, send_e, recv_e, own_e, sol_out, sol_t,
    prod, half_out, half_up, half_dn, full_up_out, full_dn_out, full_up, full_dn,
    turn, upd, own_m, send_m, recv_m, prev_out,
    sem_panel, sem_known, sem_rhs, sem_inv, sem_prev, sem_out,
    swap_send, swap_recv, b_send, b_recv, c_send, c_recv, e_send, e_recv,
    pair_send, pair_recv, s_send, s_recv,
    half_send, half_recv, full_send, full_recv, m_send, m_recv, sem_upd,
):
    i = lax.axis_index("row")
    j = lax.axis_index("col")
    z = lax.div(i, 2)
    core = lax.rem(i, 2)
    mate = i + 1 - 2 * core
    z_up = lax.rem(z + 1, RING)
    z_dn = lax.rem(z + 3, RING)
    z_far = lax.rem(z + 2, RING)
    row_up = 2 * z_up + core
    row_dn = 2 * z_dn + core
    home = lax.rem(lax.div(j, 2), 2)

    def panel_load(k):
        return pltpu.make_async_copy(panel_hbm.at[k], panel.at[core, k], sem_panel.at[k])

    def known_load(h, k):
        cols = pl.ds(h * 256, 256)
        return pltpu.make_async_copy(
            known_hbm.at[k, :, cols], known.at[k, :, cols], sem_known.at[h, k]
        )

    def inv_load(b):
        cols = pl.ds(pl.multiple_of(b * SHARE, SHARE), SHARE)
        return pltpu.make_async_copy(inv_hbm.at[:, cols], inv.at[b], sem_inv.at[b])

    def prev_load(b):
        cols = pl.ds(pl.multiple_of(b * BLOCK, BLOCK), BLOCK)
        return pltpu.make_async_copy(prev_hbm.at[:, cols], prev.at[b], sem_prev.at[b])

    rhs_load = pltpu.make_async_copy(rhs_hbm, rhs, sem_rhs)

    @functools.partial(each, 0, ROUNDS)
    def _(k):
        panel_load(k).start()
        known_load(0, k).start()

    barrier = pltpu.get_barrier_semaphore()

    @functools.partial(each, 1, COLS)
    def _(d):
        pl.semaphore_signal(
            barrier, inc=1, device_id=(i, lax.rem(j + d, COLS)), device_id_type=pl.DeviceIdType.MESH
        )

    @functools.partial(each, 1, ROWS)
    def _(d):
        pl.semaphore_signal(
            barrier, inc=1, device_id=(lax.rem(i + d, ROWS), j), device_id_type=pl.DeviceIdType.MESH
        )

    @functools.partial(each, 0, ROUNDS)
    def _(k):
        known_load(1, k).start()

    rhs_load.start()
    blocks = 2 * z + 2

    @functools.partial(each, 0, blocks)
    def _(b):
        inv_load(b).start()

    @functools.partial(each, 0, j + 1)
    def _(b):
        prev_load(b).start()

    pl.semaphore_wait(barrier, COLS - 1 + ROWS - 1)

    def swap(k):
        return remote(
            panel.at[core, k], panel.at[core, k], swap_send.at[k], swap_recv.at[k], mate, j
        )

    def swap_in(k):
        other = 1 - core
        return remote(
            panel.at[other, k], panel.at[other, k], swap_send.at[k], swap_recv.at[k], mate, j
        )

    def b_copy(other):
        return remote(
            send_b.at[other], recv_b.at[j], b_send.at[other], b_recv.at[j], i, other
        )

    def b_in(other):
        return remote(
            send_b.at[other], recv_b.at[other], b_send.at[other], b_recv.at[other], i, other
        )

    for h in range(2):
        cols = pl.ds(h * 256, 256)

        def arrive(k):
            known_load(h, k).wait()
            if h == 0:
                panel_load(k).wait()
                swap(k).start()

        def product(k):
            return jnp.dot(panel[core, k], known[k, :, cols], preferred_element_type=F32)

        arrive(0)
        acc[...] = product(0)

        @functools.partial(each, 0, 10)
        def _(s):
            for u in range(3):
                arrive(3 * s + 1 + u)
            acc[...] += product(3 * s + 1) + product(3 * s + 2) + product(3 * s + 3)

        for g in range(2):
            flipped = acc[:, g * 128 : g * 128 + 128].T.astype(BF16)
            for u in range(4):
                send_b[8 * h + 4 * g + u] = flipped[u * WIDE : (u + 1) * WIDE]

        @functools.partial(each, 8 * h, 8 * h + 8)
        def _(other):
            @pl.when(other != j)
            def _():
                b_copy(other).start()

    rhs_load.wait()

    def subtract(d, total):
        other = lax.rem(j + d, COLS)
        b_in(other).wait_recv()
        return total - recv_b[other].astype(F32)

    residue = lax.fori_loop(1, COLS, subtract, rhs[...] - send_b[j].astype(F32))
    part_c[i] = residue.astype(BF16)

    def c_copy(other):
        return remote(part_c.at[i], part_c.at[i], c_send.at[other], c_recv.at[i], other, j)

    def c_in(other):
        return remote(part_c.at[other], part_c.at[other], c_send.at[other], c_recv.at[other], other, j)

    @functools.partial(each, 0, ROWS - 1 - i)
    def _(d):
        c_copy(ROWS - 1 - d).start()

    @functools.partial(each, 0, blocks)
    def _(b):
        inv_load(b).wait()

    def dot_t(left, right):
        return lax.dot_general(left, right, (((1,), (1,)), ((), ())), preferred_element_type=F32)

    def forward(d, total):
        other = i - d
        c_in(other).wait_recv()
        return total + dot_t(part_c[other], inv[other])

    forward_t = lax.fori_loop(1, i + 1, forward, dot_t(part_c[i], inv[i])).astype(BF16)

    def e_copy(chip):
        return remote(send_e.at[chip], recv_e.at[i], e_send.at[chip], e_recv.at[i], 2 * chip + home, j)

    def e_in(other):
        return remote(send_e.at[0], recv_e.at[other], e_send.at[0], e_recv.at[other], other, j)

    @functools.partial(each, 0, z + 1)
    def _(chip):
        left = jnp.dot(forward_t, inv[2 * chip], preferred_element_type=F32)
        right = jnp.dot(forward_t, inv[2 * chip + 1], preferred_element_type=F32)
        mine = jnp.logical_and(chip == z, core == home)

        @pl.when(mine)
        def _():
            own_e[:, :SHARE] = left
            own_e[:, SHARE:] = right

        @pl.when(jnp.logical_not(mine))
        def _():
            send_e[chip, :, :SHARE] = left.astype(BF16)
            send_e[chip, :, SHARE:] = right.astype(BF16)
            e_copy(chip).start()

    def pair_copy():
        return remote(
            sol_out.at[1 - core], sol_out.at[1 - core], pair_send, pair_recv, mate, j
        )

    def pair_in():
        return remote(sol_out.at[core], sol_out.at[core], pair_send, pair_recv, mate, j)

    out_last = pltpu.make_async_copy(sol_out.at[core], last_hbm, sem_out.at[0])

    def place(col):
        return lax.div(col, 4) * 2 + lax.rem(col, 2)

    def s_copy(other):
        spot = sol_t.at[place(j)]
        return remote(spot, spot, s_send.at[other], s_recv.at[place(j)], i, other)

    def s_in(slot):
        spot = sol_t.at[slot]
        return remote(spot, spot, s_send.at[0], s_recv.at[slot], i, lax.rem(j + 1, COLS))

    @pl.when(core == home)
    def _():
        own = own_e[...]

        def add_one(other, total):
            e_in(other).wait_recv()
            return total + recv_e[other].astype(F32)

        own = lax.fori_loop(2 * z, i, add_one, own)
        own = lax.fori_loop(i + 1, ROWS, add_one, own)
        sol_t[place(j)] = own.astype(BF16)

        @functools.partial(each, 1, COLS)
        def _(d):
            s_copy(lax.rem(j + d, COLS)).start()

        sol_out[0] = own[:, :SHARE]
        sol_out[1] = own[:, SHARE:]
        pair_copy().start()

    @pl.when(core != home)
    def _():
        pair_in().wait_recv()

    out_last.start()

    @functools.partial(each, 0, 8)
    def _(slot):
        @pl.when(jnp.logical_or(core != home, slot != place(j)))
        def _():
            s_in(slot).wait_recv()

    @functools.partial(each, 0, ROUNDS)
    def _(k):
        swap_in(k).wait_recv()

    def half_up_copy(t):
        return remote(
            half_out.at[t, 0:32], half_up.at[t], half_send.at[0, t], half_recv.at[0, t], row_up, j
        )

    def half_dn_copy(t):
        return remote(
            half_out.at[t, 32:64], half_dn.at[t], half_send.at[1, t], half_recv.at[1, t], row_dn, j
        )

    def full_up_copy(t):
        return remote(
            full_up_out.at[t], full_up.at[t], full_send.at[0, t], full_recv.at[0, t], row_up, j
        )

    def full_dn_copy(t):
        return remote(
            full_dn_out.at[t], full_dn.at[t], full_send.at[1, t], full_recv.at[1, t], row_dn, j
        )

    def upd_copy(t):
        k = lax.rem(t + ROUNDS - 1, ROUNDS)
        cols = pl.ds(pl.multiple_of(k * BLOCK, BLOCK), BLOCK)
        return pltpu.make_async_copy(upd.at[t], upd_hbm.at[:, cols], sem_upd.at[t])

    def rows_of(chip):
        return pl.ds(pl.multiple_of(chip * OWN, OWN), OWN)

    def first(t):
        k = lax.rem(t + ROUNDS - 1, ROUNDS)
        slot = lax.rem(t, SLOTS)
        left = sol_t[:, :, :SHARE].reshape(256, SHARE)
        right = sol_t[:, :, SHARE:].reshape(256, SHARE)
        prod[slot] = jnp.dot(left, panel[0, k], preferred_element_type=F32) + jnp.dot(
            right, panel[1, k], preferred_element_type=F32
        )
        half_out[t] = prod[slot, rows_of(z_far), :].astype(BF16)
        half_up_copy(t).start()
        half_dn_copy(t).start()

    def second(t):
        slot = lax.rem(t, SLOTS)
        half_up_copy(t).wait_recv()
        half_dn_copy(t).wait_recv()
        up = prod[slot, rows_of(z_up), :]
        full_up_out[t, 0:32] = (up[0:32] + half_up[t].astype(F32)).astype(BF16)
        full_up_out[t, 32:64] = up[32:64].astype(BF16)
        full_up_copy(t).start()
        dn = prod[slot, rows_of(z_dn), :]
        full_dn_out[t, 0:32] = dn[0:32].astype(BF16)
        full_dn_out[t, 32:64] = (dn[32:64] + half_dn[t].astype(F32)).astype(BF16)
        full_dn_copy(t).start()

    def third(t):
        k = lax.rem(t + ROUNDS - 1, ROUNDS)
        slot = lax.rem(t, SLOTS)
        block = known[k, :, pl.ds(pl.multiple_of(z * 128, 128), 128)]
        turn[...] = block.astype(F32).T
        full_up_copy(t).wait_recv()
        full_dn_copy(t).wait_recv()
        terms = prod[slot, rows_of(z), :] + full_up[t].astype(F32) + full_dn[t].astype(F32)
        upd[t] = turn[rows_of(core), :] - terms
        upd_copy(t).start()

    def step(t):
        @pl.when(t < ROUNDS)
        def _():
            first(t)

        @pl.when(jnp.logical_and(t >= LAG_ADD, t < ROUNDS + LAG_ADD))
        def _():
            second(t - LAG_ADD)

        @pl.when(t >= LAG_END)
        def _():
            third(t - LAG_END)

    each(0, LAG_END + 1, step)

    def m_copy(other):
        return remote(send_m.at[other], recv_m.at[j], m_send.at[other], m_recv.at[j], i, other)

    def m_in(other):
        return remote(send_m.at[other], recv_m.at[other], m_send.at[other], m_recv.at[other], i, other)

    @functools.partial(each, 0, j + 1)
    def _(b):
        prev_load(b).wait()

    prior = upd[0].astype(BF16)
    own_m[...] = jnp.dot(prior, prev[j], preferred_element_type=F32)

    @functools.partial(each, 0, j)
    def _(b):
        send_m[b] = jnp.dot(prior, prev[b], preferred_element_type=F32).astype(BF16)
        m_copy(b).start()

    each(LAG_END + 1, ROUNDS + LAG_END, step)

    def add_m(other, total):
        m_in(other).wait_recv()
        return total + recv_m[other].astype(F32)

    prev_out[...] = lax.fori_loop(j + 1, COLS, add_m, own_m[...])
    out_prev = pltpu.make_async_copy(prev_out, sol_prev_hbm, sem_out.at[1])
    out_prev.start()

    @functools.partial(each, 0, COLS)
    def _(other):
        @pl.when(other != j)
        def _():
            b_copy(other).wait_send()

            @pl.when(core == home)
            def _():
                s_copy(other).wait_send()

    @functools.partial(each, 0, ROWS - 1 - i)
    def _(d):
        c_copy(ROWS - 1 - d).wait_send()

    @functools.partial(each, 0, z + 1)
    def _(chip):
        @pl.when(jnp.logical_not(jnp.logical_and(chip == z, core == home)))
        def _():
            e_copy(chip).wait_send()

    @pl.when(core == home)
    def _():
        pair_copy().wait_send()

    @functools.partial(each, 0, j)
    def _(b):
        m_copy(b).wait_send()

    @functools.partial(each, 0, ROUNDS)
    def _(t):
        swap(t).wait_send()
        half_up_copy(t).wait_send()
        half_dn_copy(t).wait_send()
        full_up_copy(t).wait_send()
        full_dn_copy(t).wait_send()
        upd_copy(t).wait()

    out_last.wait()
    out_prev.wait()


def scratch():
    dma = pltpu.SemaphoreType.DMA
    return [
        pltpu.VMEM((2, ROUNDS, SHARE, BLOCK), BF16),
        pltpu.VMEM((ROUNDS, BLOCK, SIDES), BF16),
        pltpu.VMEM((WIDE, SHARE), F32),
        pltpu.VMEM((ROWS, SHARE, SHARE), BF16),
        pltpu.VMEM((COLS, BLOCK, BLOCK), BF16),
        pltpu.VMEM((SHARE, 256), F32),
        pltpu.VMEM((COLS, WIDE, SHARE), BF16),
        pltpu.VMEM((COLS, WIDE, SHARE), BF16),
        pltpu.VMEM((ROWS, WIDE, SHARE), BF16),
        pltpu.VMEM((RING, WIDE, 2 * SHARE), BF16),
        pltpu.VMEM((ROWS, WIDE, 2 * SHARE), BF16),
        pltpu.VMEM((WIDE, 2 * SHARE), F32),
        pltpu.VMEM((2, WIDE, SHARE), F32),
        pltpu.VMEM((8, WIDE, 2 * SHARE), BF16),
        pltpu.VMEM((SLOTS, 256, BLOCK), F32),
        pltpu.VMEM((ROUNDS, OWN, BLOCK), BF16),
        pltpu.VMEM((ROUNDS, OWN // 2, BLOCK), BF16),
        pltpu.VMEM((ROUNDS, OWN // 2, BLOCK), BF16),
        pltpu.VMEM((ROUNDS, OWN, BLOCK), BF16),
        pltpu.VMEM((ROUNDS, OWN, BLOCK), BF16),
        pltpu.VMEM((ROUNDS, OWN, BLOCK), BF16),
        pltpu.VMEM((ROUNDS, OWN, BLOCK), BF16),
        pltpu.VMEM((128, BLOCK), F32),
        pltpu.VMEM((ROUNDS, OWN, BLOCK), F32),
        pltpu.VMEM((OWN, BLOCK), F32),
        pltpu.VMEM((COLS, OWN, BLOCK), BF16),
        pltpu.VMEM((COLS, OWN, BLOCK), BF16),
        pltpu.VMEM((OWN, BLOCK), F32),
        dma((ROUNDS,)),
        dma((2, ROUNDS)),
        dma(()),
        dma((ROWS,)),
        dma((COLS,)),
        dma((2,)),
        dma((ROUNDS,)),
        dma((ROUNDS,)),
        dma((COLS,)),
        dma((COLS,)),
        dma((ROWS,)),
        dma((ROWS,)),
        dma((RING,)),
        dma((ROWS,)),
        dma(()),
        dma(()),
        dma((COLS,)),
        dma((8,)),
        dma((2, ROUNDS)),
        dma((2, ROUNDS)),
        dma((2, ROUNDS)),
        dma((2, ROUNDS)),
        dma((COLS,)),
        dma((COLS,)),
        dma((ROUNDS,)),
    ]


def per_device(factor_panel, solved_prev, rhs_last, inv_last, inv_prev):
    panel = factor_panel.transpose(1, 2, 0, 3).reshape(ROUNDS, SHARE, BLOCK)
    known = solved_prev.reshape(ROUNDS, BLOCK, SIDES)
    anywhere = pl.BlockSpec(memory_space=pl.ANY)
    updated, last_t, prev_t = pl.pallas_call(
        kernel,
        out_shape=[
            jax.ShapeDtypeStruct((OWN, ROUNDS * BLOCK), F32),
            jax.ShapeDtypeStruct((WIDE, SHARE), F32),
            jax.ShapeDtypeStruct((OWN, BLOCK), F32),
        ],
        in_specs=[anywhere] * 5,
        out_specs=[anywhere] * 3,
        scratch_shapes=scratch(),
        compiler_params=pltpu.CompilerParams(
            collective_id=0, has_side_effects=True, vmem_limit_bytes=60 * 1024 * 1024
        ),
        cost_estimate=pl.CostEstimate(
            flops=9 * 10**9, bytes_accessed=21 * 10**6, transcendentals=0
        ),
    )(panel, known, rhs_last.T, inv_last, inv_prev.reshape(BLOCK, COLS * BLOCK))
    return updated.reshape(OWN, ROUNDS, 1, BLOCK), last_t.T, prev_t.T


def solution(mesh):
    in_specs = (
        P("row", None, "col", None),
        P(None, "col", None, None),
        P("row", "col"),
        P("row", None),
        P(None, "col", None, None),
    )
    out_specs = (P("row", None, "col", None), P("row", "col"), P("col", "row"))
    return jax.shard_map(
        per_device, mesh=mesh, in_specs=in_specs, out_specs=out_specs, check_vma=False
    )
```

```python
import functools

import jax
import jax.numpy as jnp
from jax import lax
from jax.experimental import pallas as pl
from jax.experimental.pallas import tpu as pltpu
from jax.sharding import PartitionSpec as P

ROWS = 8
COLS = 16
RING = 4
ROUNDS = 31
SIDES = 512
SHARE = 512
BLOCK = 256
WIDE = 32
OWN = 64
GROUP = 6
STEPS = 2 * ROUNDS
AHEAD = 12
LAG_ADD = 6
LAG_END = 12
SLOTS = LAG_END + 2
PIECES = 4
GROUPS = 5
F32 = jnp.float32
BF16 = jnp.bfloat16


def remote(src, dst, send_sem, recv_sem, row, col):
    return pltpu.make_async_remote_copy(
        src_ref=src,
        dst_ref=dst,
        send_sem=send_sem,
        recv_sem=recv_sem,
        device_id=(row, col),
        device_id_type=pl.DeviceIdType.MESH,
    )


def each(start, stop, body):
    def step(index, carry):
        body(index)
        return carry

    lax.fori_loop(start, stop, step, 0)


def kernel(
    panel_hbm, known_hbm, rhs_hbm, inv_hbm, prev_hbm,
    upd_hbm, last_hbm, sol_prev_hbm,
    panel, known, rhs, inv, prev,
    acc, send_b, recv_b, part_c, send_e, recv_e, own_e, sol_out, sol_t,
    prod, half_out, half_in, full_out, full_in,
    turn, begin, upd, prior, own_m, send_m, recv_m, prev_out,
    sem_panel, sem_known, sem_rhs, sem_inv, sem_prev, sem_out,
    swap_send, swap_recv, b_send, b_recv, c_send, c_recv, e_send, e_recv,
    pair_send, pair_recv, s_send, s_recv,
    half_send, half_recv, full_send, full_recv, m_send, m_recv, sem_upd,
):
    i = lax.axis_index("row")
    j = lax.axis_index("col")
    z = lax.div(i, 2)
    core = lax.rem(i, 2)
    mate = i + 1 - 2 * core
    z_up = lax.rem(z + 1, RING)
    z_dn = lax.rem(z + 3, RING)
    z_far = lax.rem(z + 2, RING)
    row_up = 2 * z_up + core
    row_dn = 2 * z_dn + core
    home = lax.rem(lax.div(j, 2), 2)

    def span(g):
        return pl.ds((ROUNDS - 1) if isinstance(g, str) else g * GROUP, 1 if isinstance(g, str) else GROUP)

    def sem_of(g):
        return GROUPS if isinstance(g, str) else g

    def panel_load(h, g):
        rows = pl.ds(h * 256, 256)
        return pltpu.make_async_copy(
            panel_hbm.at[span(g), rows],
            panel.at[core, span(g), rows],
            sem_panel.at[h, sem_of(g)],
        )

    def known_load(g):
        return pltpu.make_async_copy(
            known_hbm.at[span(g)], known.at[span(g)], sem_known.at[sem_of(g)]
        )

    inv_load = pltpu.make_async_copy(inv_hbm, inv, sem_inv)
    prev_load = pltpu.make_async_copy(prev_hbm, prev, sem_prev)
    rhs_load = pltpu.make_async_copy(rhs_hbm, rhs, sem_rhs)

    panel_load(0, "last").start()
    known_load("last").start()

    @functools.partial(each, 0, GROUPS)
    def _(g):
        panel_load(0, g).start()
        known_load(g).start()

    barrier = pltpu.get_barrier_semaphore()

    @functools.partial(each, 1, COLS)
    def _(d):
        pl.semaphore_signal(
            barrier, inc=1, device_id=(i, lax.rem(j + d, COLS)), device_id_type=pl.DeviceIdType.MESH
        )

    @functools.partial(each, 1, ROWS)
    def _(d):
        pl.semaphore_signal(
            barrier, inc=1, device_id=(lax.rem(i + d, ROWS), j), device_id_type=pl.DeviceIdType.MESH
        )

    panel_load(1, "last").start()

    @functools.partial(each, 0, GROUPS)
    def _(g):
        panel_load(1, g).start()

    rhs_load.start()

    def swap(h, g):
        spot = panel.at[core, span(g), pl.ds(h * 256, 256)]
        return remote(spot, spot, swap_send, swap_recv.at[sem_of(g)], mate, j)

    def swap_in(g):
        spot = panel.at[1 - core, span(g)]
        return remote(spot, spot, swap_send, swap_recv.at[sem_of(g)], mate, j)

    def swap_all():
        return remote(panel.at[core], panel.at[core], swap_send, swap_recv.at[0], mate, j)

    def b_copy(h, other):
        return remote(
            send_b.at[h, other], recv_b.at[h, j], b_send, b_recv.at[h], i, other
        )

    def b_all(h):
        rest = pl.ds(0, COLS - 1)
        return remote(
            send_b.at[h, rest], recv_b.at[h, rest], b_send, b_recv.at[h], i, lax.rem(j + 1, COLS)
        )

    for h in range(2):
        rows = pl.ds(h * 256, 256)

        def arrive(g):
            panel_load(h, g).wait()
            if h == 0:
                known_load(g).wait()
            else:
                swap(1, g).start()

        def product(k):
            return jnp.dot(panel[core, k, rows], known[k], preferred_element_type=F32)

        arrive("last")
        acc[...] = product(ROUNDS - 1)

        @functools.partial(each, 0, GROUPS)
        def _(g):
            arrive(g)
            total = product(GROUP * g)
            for u in range(1, GROUP):
                total = total + product(GROUP * g + u)
            acc[...] += total

        for g in range(4):
            flipped = acc[:, g * 128 : g * 128 + 128].T.astype(BF16)
            for u in range(4):
                send_b[h, 4 * g + u] = flipped[u * WIDE : (u + 1) * WIDE]

        if h == 0:
            pl.semaphore_wait(barrier, COLS - 1 + ROWS - 1)

        for odd in range(2):

            @functools.partial(each, 0, COLS // 2)
            def _(half):
                other = 2 * half + odd

                @pl.when(other != j)
                def _():
                    b_copy(h, other).start()

        if h == 0:
            swap(0, "last").start()

            @functools.partial(each, 0, GROUPS)
            def _(g):
                swap(0, g).start()

            inv_load.start()
            prev_load.start()

    rhs_load.wait()

    for h in range(2):
        rows = pl.ds(h * 256, 256)

        def subtract(d, total):
            other = lax.rem(j + d, COLS)
            return total - recv_b[h, other].astype(F32)

        b_all(h).wait_recv()
        residue = lax.fori_loop(1, COLS, subtract, rhs[:, rows] - send_b[h, j].astype(F32))
        part_c[i, :, rows] = residue.astype(BF16)

    def c_copy(other):
        return remote(part_c.at[i], part_c.at[i], c_send.at[other], c_recv.at[i], other, j)

    def c_in(other):
        return remote(part_c.at[other], part_c.at[other], c_send.at[other], c_recv.at[other], other, j)

    @functools.partial(each, 0, ROWS - 1 - i)
    def _(d):
        c_copy(ROWS - 1 - d).start()

    inv_load.wait()

    def inv_block(b):
        return inv[:, pl.ds(pl.multiple_of(b * SHARE, SHARE), SHARE)]

    def dot_t(left, right):
        return lax.dot_general(left, right, (((1,), (1,)), ((), ())), preferred_element_type=F32)

    def forward(d, total):
        other = i - d
        c_in(other).wait_recv()
        return total + dot_t(part_c[other], inv_block(other))

    forward_t = lax.fori_loop(1, i + 1, forward, dot_t(part_c[i], inv_block(i))).astype(BF16)

    def e_copy(chip):
        return remote(send_e.at[chip], recv_e.at[i], e_send.at[chip], e_recv.at[i], 2 * chip + home, j)

    def e_in(other):
        return remote(send_e.at[0], recv_e.at[other], e_send.at[0], e_recv.at[other], other, j)

    @functools.partial(each, 0, z + 1)
    def _(chip):
        left = jnp.dot(forward_t, inv_block(2 * chip), preferred_element_type=F32)
        right = jnp.dot(forward_t, inv_block(2 * chip + 1), preferred_element_type=F32)
        mine = jnp.logical_and(chip == z, core == home)

        @pl.when(mine)
        def _():
            own_e[:, :SHARE] = left
            own_e[:, SHARE:] = right

        @pl.when(jnp.logical_not(mine))
        def _():
            send_e[chip, :, :SHARE] = left.astype(BF16)
            send_e[chip, :, SHARE:] = right.astype(BF16)
            e_copy(chip).start()

    def pair_copy():
        return remote(
            sol_out.at[1 - core], sol_out.at[1 - core], pair_send, pair_recv, mate, j
        )

    def pair_in():
        return remote(sol_out.at[core], sol_out.at[core], pair_send, pair_recv, mate, j)

    out_last = pltpu.make_async_copy(sol_out.at[core], last_hbm, sem_out.at[0])

    my_set = lax.rem(j, 2)
    my_chip = lax.div(j, 4)

    def s_copy(other):
        spot = sol_t.at[my_set, my_chip]
        return remote(spot, spot, s_send, s_recv.at[my_set, my_chip], i, other)

    def s_in(side, chip):
        spot = sol_t.at[side, chip]
        return remote(
            spot, spot, s_send, s_recv.at[side, chip], i, lax.rem(j + 1, COLS)
        )

    @pl.when(core == home)
    def _():
        own = own_e[...]

        def add_one(other, total):
            e_in(other).wait_recv()
            return total + recv_e[other].astype(F32)

        own = lax.fori_loop(2 * z, i, add_one, own)
        own = lax.fori_loop(i + 1, ROWS, add_one, own)
        sol_t[my_set, my_chip] = own.astype(BF16)

        @functools.partial(each, 1, COLS)
        def _(d):
            s_copy(lax.rem(j + d, COLS)).start()

        sol_out[0] = own[:, :SHARE]
        sol_out[1] = own[:, SHARE:]
        pair_copy().start()

    @pl.when(core != home)
    def _():
        pair_in().wait_recv()

    out_last.start()

    def solved(side):
        @functools.partial(each, 0, RING)
        def _(chip):
            @pl.when((core != home) | (my_set != side) | (my_chip != chip))
            def _():
                s_in(side, chip).wait_recv()

    def half_copy(t, up):
        n = lax.rem(t, SLOTS)
        return remote(
            half_out.at[n, up], half_in.at[n, up], half_send.at[n], half_recv.at[n],
            row_up if up else row_dn, j,
        )

    def half_both(t):
        n = lax.rem(t, SLOTS)
        return remote(half_out.at[n], half_in.at[n], half_send.at[n], half_recv.at[n], row_up, j)

    def full_copy(t, up):
        n = lax.rem(t, SLOTS)
        return remote(
            full_out.at[n, up], full_in.at[n, up], full_send.at[n], full_recv.at[n],
            row_up if up else row_dn, j,
        )

    def full_both(t):
        n = lax.rem(t, SLOTS)
        return remote(full_out.at[n], full_in.at[n], full_send.at[n], full_recv.at[n], row_up, j)

    def side_of(t):
        late = lax.rem(lax.max(t - 2 * AHEAD, 0), 2)
        return jnp.where(t < 2 * AHEAD, lax.div(t, AHEAD), late)

    def spot_of(t):
        late = AHEAD + lax.div(lax.max(t - 2 * AHEAD, 0), 2)
        return jnp.where(t < 2 * AHEAD, lax.rem(t, AHEAD), late)

    def round_of(spot):
        return lax.rem(spot + ROUNDS - 1, ROUNDS)

    def sides_of(side):
        return pl.ds(pl.multiple_of(side * WIDE, WIDE), WIDE)

    def rows_of(chip):
        return pl.ds(pl.multiple_of(chip * WIDE, WIDE), WIDE)

    def swapped(t):
        spot = spot_of(t)

        @pl.when(spot == 0)
        def _():
            swap_in("last").wait_recv()

        @pl.when((spot > 0) & (lax.rem(spot + GROUP - 1, GROUP) == 0))
        def _():
            swap_in(lax.div(spot - 1, GROUP)).wait_recv()

    def multiply(t, side):
        k = round_of(spot_of(t))
        left = sol_t[side, :, :, :SHARE].reshape(RING * WIDE, SHARE)
        right = sol_t[side, :, :, SHARE:].reshape(RING * WIDE, SHARE)
        return jnp.dot(left, panel[0, k], preferred_element_type=F32) + jnp.dot(
            right, panel[1, k], preferred_element_type=F32
        )

    def multiply_both(t):
        k = round_of(spot_of(t))
        left = sol_t[:, :, :, :SHARE].reshape(2 * RING * WIDE, SHARE)
        right = sol_t[:, :, :, SHARE:].reshape(2 * RING * WIDE, SHARE)
        return jnp.dot(left, panel[0, k], preferred_element_type=F32) + jnp.dot(
            right, panel[1, k], preferred_element_type=F32
        )

    def first(t):
        n = lax.rem(t, SLOTS)

        @pl.when(side_of(t) == 0)
        def _():
            swapped(t)

        @pl.when(t < 2 * AHEAD)
        def _():
            prod[n] = multiply(t, side_of(t))

        @pl.when((t >= 2 * AHEAD) & (side_of(t) == 0))
        def _():
            both = multiply_both(t)
            prod[n] = both[: RING * WIDE]
            prod[lax.rem(t + 1, SLOTS)] = both[RING * WIDE :]

        @pl.when(t >= SLOTS)
        def _():
            half_both(t).wait_send()

        far = prod[n, rows_of(z_far), :].astype(BF16)
        half_out[n, 1] = far[:16]
        half_out[n, 0] = far[16:]
        half_copy(t, 1).start()
        half_copy(t, 0).start()

    def second(t):
        n = lax.rem(t, SLOTS)
        half_both(t).wait_recv()

        @pl.when(t >= SLOTS)
        def _():
            full_both(t).wait_send()

        up = prod[n, rows_of(z_up), :]
        full_out[n, 1, 0:16] = (up[0:16] + half_in[n, 1].astype(F32)).astype(BF16)
        full_out[n, 1, 16:32] = up[16:32].astype(BF16)
        full_copy(t, 1).start()
        dn = prod[n, rows_of(z_dn), :]
        full_out[n, 0, 0:16] = dn[0:16].astype(BF16)
        full_out[n, 0, 16:32] = (dn[16:32] + half_in[n, 0].astype(F32)).astype(BF16)
        full_copy(t, 0).start()

    def third(t):
        side, spot = side_of(t), spot_of(t)
        k = round_of(spot)
        n = lax.rem(t, SLOTS)

        @pl.when(side == 0)
        def _():
            block = known[k, :, pl.ds(pl.multiple_of(z * 128, 128), 128)]
            turn[...] = block.astype(F32).T
            begin[spot] = turn[pl.ds(pl.multiple_of(core * OWN, OWN), OWN), :]

        full_both(t).wait_recv()
        sides = sides_of(side)
        terms = prod[n, rows_of(z), :] + full_in[n, 1].astype(F32) + full_in[n, 0].astype(F32)
        done = begin[spot, sides, :] - terms
        for part in range(2):
            where = side * (WIDE * 2 * ROUNDS) + 2 * k + part
            upd[pl.ds(where, WIDE, stride=2 * ROUNDS), :] = done[:, part * 128 : part * 128 + 128]

        @pl.when(spot == 0)
        def _():
            prior[sides, :] = done.astype(BF16)

    def step(t):
        @pl.when(t < STEPS)
        def _():
            first(t)

        @pl.when(jnp.logical_and(t >= LAG_ADD, t < STEPS + LAG_ADD))
        def _():
            second(t - LAG_ADD)

        @pl.when(t >= LAG_END)
        def _():
            third(t - LAG_END)

    solved(0)
    each(0, AHEAD, step)
    solved(1)
    each(AHEAD, AHEAD + LAG_END + 1, step)

    def m_copy(other):
        return remote(send_m.at[other], recv_m.at[j], m_send.at[other], m_recv.at[j], i, other)

    def m_in(other):
        return remote(send_m.at[other], recv_m.at[other], m_send.at[other], m_recv.at[other], i, other)

    prev_load.wait()

    def prev_block(b):
        return prev[:, pl.ds(pl.multiple_of(b * BLOCK, BLOCK), BLOCK)]

    own_m[...] = jnp.dot(prior[...], prev_block(j), preferred_element_type=F32)

    @functools.partial(each, 0, j)
    def _(b):
        send_m[b] = jnp.dot(prior[...], prev_block(b), preferred_element_type=F32).astype(BF16)
        m_copy(b).start()

    each(AHEAD + LAG_END + 1, STEPS + LAG_END, step)

    out_upd = pltpu.make_async_copy(upd, upd_hbm, sem_upd)
    out_upd.start()

    def add_m(other, total):
        m_in(other).wait_recv()
        return total + recv_m[other].astype(F32)

    prev_out[...] = lax.fori_loop(j + 1, COLS, add_m, own_m[...])
    out_prev = pltpu.make_async_copy(prev_out, sol_prev_hbm, sem_out.at[1])
    out_prev.start()

    b_all(0).wait_send()
    b_all(1).wait_send()
    swap_all().wait_send()

    @functools.partial(each, 0, ROWS - 1 - i)
    def _(d):
        c_copy(ROWS - 1 - d).wait_send()

    @functools.partial(each, 0, z + 1)
    def _(chip):
        @pl.when(jnp.logical_not(jnp.logical_and(chip == z, core == home)))
        def _():
            e_copy(chip).wait_send()

    @pl.when(core == home)
    def _():
        pair_copy().wait_send()

        @functools.partial(each, 1, COLS)
        def _(d):
            s_copy(lax.rem(j + d, COLS)).wait_send()

    @functools.partial(each, 0, j)
    def _(b):
        m_copy(b).wait_send()

    @functools.partial(each, STEPS - SLOTS, STEPS)
    def _(t):
        half_both(t).wait_send()
        full_both(t).wait_send()

    out_upd.wait()
    out_last.wait()
    out_prev.wait()


def hand_over(upd_in, last_in, prev_in, upd_out, last_out, prev_out, upd, last, prev, sems):
    def piece(ref, n):
        rows = ref.shape[0] // PIECES
        return ref.at[pl.ds(n * rows, rows)]

    moves = [(last_in, last, last_out), (prev_in, prev, prev_out)]
    moves += [(piece(upd_in, n), piece(upd, n), piece(upd_out, n)) for n in range(PIECES)]
    loads = [pltpu.make_async_copy(a, b, sems.at[0, n]) for n, (a, b, _) in enumerate(moves)]
    stores = [pltpu.make_async_copy(b, c, sems.at[1, n]) for n, (_, b, c) in enumerate(moves)]
    for load in loads:
        load.start()
    for load, store in zip(loads, stores):
        load.wait()
        store.start()
    for store in stores:
        store.wait()


def scratch():
    dma = pltpu.SemaphoreType.DMA
    return [
        pltpu.VMEM((2, ROUNDS, SHARE, BLOCK), BF16),
        pltpu.VMEM((ROUNDS, BLOCK, SIDES), BF16),
        pltpu.VMEM((WIDE, SHARE), F32),
        pltpu.VMEM((SHARE, ROWS * SHARE), BF16),
        pltpu.VMEM((BLOCK, COLS * BLOCK), BF16),
        pltpu.VMEM((256, SIDES), F32),
        pltpu.VMEM((2, COLS, WIDE, 256), BF16),
        pltpu.VMEM((2, COLS, WIDE, 256), BF16),
        pltpu.VMEM((ROWS, WIDE, SHARE), BF16),
        pltpu.VMEM((RING, WIDE, 2 * SHARE), BF16),
        pltpu.VMEM((ROWS, WIDE, 2 * SHARE), BF16),
        pltpu.VMEM((WIDE, 2 * SHARE), F32),
        pltpu.VMEM((2, WIDE, SHARE), F32),
        pltpu.VMEM((2, RING, WIDE, 2 * SHARE), BF16),
        pltpu.VMEM((SLOTS, RING * WIDE, BLOCK), F32),
        pltpu.VMEM((SLOTS, 2, WIDE // 2, BLOCK), BF16),
        pltpu.VMEM((SLOTS, 2, WIDE // 2, BLOCK), BF16),
        pltpu.VMEM((SLOTS, 2, WIDE, BLOCK), BF16),
        pltpu.VMEM((SLOTS, 2, WIDE, BLOCK), BF16),
        pltpu.VMEM((128, BLOCK), F32),
        pltpu.VMEM((ROUNDS, OWN, BLOCK), F32),
        pltpu.VMEM((OWN * ROUNDS * 2, 128), F32),
        pltpu.VMEM((OWN, BLOCK), BF16),
        pltpu.VMEM((OWN, BLOCK), F32),
        pltpu.VMEM((COLS, OWN, BLOCK), BF16),
        pltpu.VMEM((COLS, OWN, BLOCK), BF16),
        pltpu.VMEM((OWN, BLOCK), F32),
        dma((2, GROUPS + 1)),
        dma((GROUPS + 1,)),
        dma(()),
        dma(()),
        dma(()),
        dma((2,)),
        dma(()),
        dma((GROUPS + 1,)),
        dma(()),
        dma((2,)),
        dma((ROWS,)),
        dma((ROWS,)),
        dma((RING,)),
        dma((ROWS,)),
        dma(()),
        dma(()),
        dma(()),
        dma((2, RING)),
        dma((SLOTS,)),
        dma((SLOTS,)),
        dma((SLOTS,)),
        dma((SLOTS,)),
        dma((COLS,)),
        dma((COLS,)),
        dma(()),
    ]


def per_device(factor_panel, solved_prev, rhs_last, inv_last, inv_prev):
    panel = factor_panel.transpose(1, 2, 0, 3).reshape(ROUNDS, SHARE, BLOCK)
    known = solved_prev.reshape(ROUNDS, BLOCK, SIDES)
    anywhere = pl.BlockSpec(memory_space=pl.ANY)
    out_shape = [
        jax.ShapeDtypeStruct((OWN * ROUNDS * 2, 128), F32),
        jax.ShapeDtypeStruct((WIDE, SHARE), F32),
        jax.ShapeDtypeStruct((OWN, BLOCK), F32),
    ]
    results = pl.pallas_call(
        kernel,
        out_shape=out_shape,
        in_specs=[anywhere] * 5,
        out_specs=[anywhere] * 3,
        scratch_shapes=scratch(),
        compiler_params=pltpu.CompilerParams(
            collective_id=0, has_side_effects=True, vmem_limit_bytes=60 * 1024 * 1024
        ),
        cost_estimate=pl.CostEstimate(
            flops=9 * 10**9, bytes_accessed=21 * 10**6, transcendentals=0
        ),
    )(panel, known, rhs_last.T, inv_last, inv_prev.reshape(BLOCK, COLS * BLOCK))
    updated, last_t, prev_t = pl.pallas_call(
        hand_over,
        out_shape=out_shape,
        in_specs=[anywhere] * 3,
        out_specs=[anywhere] * 3,
        scratch_shapes=[pltpu.VMEM(shape.shape, shape.dtype) for shape in out_shape]
        + [pltpu.SemaphoreType.DMA((2, PIECES + 2))],
        compiler_params=pltpu.CompilerParams(vmem_limit_bytes=60 * 1024 * 1024),
    )(*results)
    return updated.reshape(OWN, ROUNDS, 1, BLOCK), last_t.T, prev_t.T


def solution(mesh):
    in_specs = (
        P("row", None, "col", None),
        P(None, "col", None, None),
        P("row", "col"),
        P("row", None),
        P(None, "col", None, None),
    )
    out_specs = (P("row", None, "col", None), P("row", "col"), P("col", "row"))
    return jax.shard_map(
        per_device, mesh=mesh, in_specs=in_specs, out_specs=out_specs, check_vma=False
    )
```

```python
import functools

import jax
import jax.numpy as jnp
from jax import lax
from jax.experimental import pallas as pl
from jax.experimental.pallas import tpu as pltpu
from jax.sharding import PartitionSpec as P

ROWS = 8
COLS = 16
RING = 4
ROUNDS = 31
SIDES = 512
SHARE = 512
BLOCK = 256
WIDE = 32
OWN = 64
GROUP = 6
STEPS = 2 * ROUNDS
AHEAD = 12
LAG_ADD = 10
LAG_END = 20
SLOTS = LAG_END + 2
PIECES = 4
GROUPS = 5
F32 = jnp.float32
BF16 = jnp.bfloat16


def remote(src, dst, send_sem, recv_sem, row, col):
    return pltpu.make_async_remote_copy(
        src_ref=src,
        dst_ref=dst,
        send_sem=send_sem,
        recv_sem=recv_sem,
        device_id=(row, col),
        device_id_type=pl.DeviceIdType.MESH,
    )


def each(start, stop, body):
    def step(index, carry):
        body(index)
        return carry

    lax.fori_loop(start, stop, step, 0)


def kernel(
    panel_hbm, known_hbm, rhs_hbm, inv_hbm, prev_hbm,
    upd_hbm, last_hbm, sol_prev_hbm,
    panel, known, rhs, inv, prev,
    acc, send_b, recv_b, part_c, send_e, recv_e, own_e, sol_out, sol_t,
    prod, half_out, half_in, full_out, full_in,
    turn, begin, upd, prior, own_m, send_m, recv_m, prev_out,
    sem_panel, sem_known, sem_rhs, sem_inv, sem_prev, sem_out,
    swap_send, swap_recv, b_send, b_recv, c_send, c_recv, e_send, e_recv,
    pair_send, pair_recv, s_send, s_recv,
    half_send, half_recv, full_send, full_recv, m_send, m_recv, sem_upd,
):
    i = lax.axis_index("row")
    j = lax.axis_index("col")
    z = lax.div(i, 2)
    core = lax.rem(i, 2)
    mate = i + 1 - 2 * core
    z_up = lax.rem(z + 1, RING)
    z_dn = lax.rem(z + 3, RING)
    z_far = lax.rem(z + 2, RING)
    row_up = 2 * z_up + core
    row_dn = 2 * z_dn + core
    home = lax.rem(lax.div(j, 2), 2)

    def span(g):
        return pl.ds((ROUNDS - 1) if isinstance(g, str) else g * GROUP, 1 if isinstance(g, str) else GROUP)

    def sem_of(g):
        return GROUPS if isinstance(g, str) else g

    def panel_load(h, g):
        rows = pl.ds(h * 256, 256)
        return pltpu.make_async_copy(
            panel_hbm.at[span(g), rows],
            panel.at[core, span(g), rows],
            sem_panel.at[h, sem_of(g)],
        )

    def known_load(g):
        return pltpu.make_async_copy(
            known_hbm.at[span(g)], known.at[span(g)], sem_known.at[sem_of(g)]
        )

    inv_load = pltpu.make_async_copy(inv_hbm, inv, sem_inv)
    prev_load = pltpu.make_async_copy(prev_hbm, prev, sem_prev)
    rhs_load = pltpu.make_async_copy(rhs_hbm, rhs, sem_rhs)

    panel_load(0, "last").start()
    known_load("last").start()

    @functools.partial(each, 0, GROUPS)
    def _(g):
        panel_load(0, g).start()
        known_load(g).start()

    barrier = pltpu.get_barrier_semaphore()

    @functools.partial(each, 1, COLS)
    def _(d):
        pl.semaphore_signal(
            barrier, inc=1, device_id=(i, lax.rem(j + d, COLS)), device_id_type=pl.DeviceIdType.MESH
        )

    @functools.partial(each, 1, ROWS)
    def _(d):
        pl.semaphore_signal(
            barrier, inc=1, device_id=(lax.rem(i + d, ROWS), j), device_id_type=pl.DeviceIdType.MESH
        )

    panel_load(1, "last").start()

    @functools.partial(each, 0, GROUPS)
    def _(g):
        panel_load(1, g).start()

    rhs_load.start()

    def swap(h, g):
        spot = panel.at[core, span(g), pl.ds(h * 256, 256)]
        return remote(spot, spot, swap_send, swap_recv.at[sem_of(g)], mate, j)

    def swap_in(g):
        spot = panel.at[1 - core, span(g)]
        return remote(spot, spot, swap_send, swap_recv.at[sem_of(g)], mate, j)

    def swap_all():
        return remote(panel.at[core], panel.at[core], swap_send, swap_recv.at[0], mate, j)

    def b_copy(h, other):
        return remote(
            send_b.at[h, other], recv_b.at[h, j], b_send, b_recv.at[h], i, other
        )

    def b_all(h):
        rest = pl.ds(0, COLS - 1)
        return remote(
            send_b.at[h, rest], recv_b.at[h, rest], b_send, b_recv.at[h], i, lax.rem(j + 1, COLS)
        )

    for h in range(2):
        rows = pl.ds(h * 256, 256)

        def arrive(g):
            panel_load(h, g).wait()
            if h == 0:
                known_load(g).wait()
            else:
                swap(1, g).start()

        def product(k):
            return jnp.dot(panel[core, k, rows], known[k], preferred_element_type=F32)

        arrive("last")
        acc[...] = product(ROUNDS - 1)

        @functools.partial(each, 0, GROUPS)
        def _(g):
            arrive(g)
            total = product(GROUP * g)
            for u in range(1, GROUP):
                total = total + product(GROUP * g + u)
            acc[...] += total

        for g in range(4):
            flipped = acc[:, g * 128 : g * 128 + 128].T.astype(BF16)
            for u in range(4):
                send_b[h, 4 * g + u] = flipped[u * WIDE : (u + 1) * WIDE]

        if h == 0:
            pl.semaphore_wait(barrier, COLS - 1 + ROWS - 1)

        for odd in range(2):

            @functools.partial(each, 0, COLS // 2)
            def _(half):
                x = lax.rem(lax.div(j, 4) + lax.div(half, 2), 4)
                y = lax.rem(lax.rem(j, 4) + 2 * lax.rem(half, 2), 4)
                other = 4 * x + y + lax.rem(x + y + odd, 2) * (1 - 2 * lax.rem(y, 2))

                @pl.when(other != j)
                def _():
                    b_copy(h, other).start()

        if h == 0:
            swap(0, "last").start()

            @functools.partial(each, 0, GROUPS)
            def _(g):
                swap(0, g).start()

            inv_load.start()
            prev_load.start()

    rhs_load.wait()

    for h in range(2):
        rows = pl.ds(h * 256, 256)

        def subtract(d, total):
            other = lax.rem(j + d, COLS)
            return total - recv_b[h, other].astype(F32)

        b_all(h).wait_recv()
        residue = lax.fori_loop(1, COLS, subtract, rhs[:, rows] - send_b[h, j].astype(F32))
        part_c[i, :, rows] = residue.astype(BF16)

    def c_copy(other):
        return remote(part_c.at[i], part_c.at[i], c_send.at[other], c_recv.at[i], other, j)

    def c_in(other):
        return remote(part_c.at[other], part_c.at[other], c_send.at[other], c_recv.at[other], other, j)

    @functools.partial(each, 0, ROWS - 1 - i)
    def _(d):
        c_copy(ROWS - 1 - d).start()

    inv_load.wait()

    def inv_block(b):
        return inv[:, pl.ds(pl.multiple_of(b * SHARE, SHARE), SHARE)]

    def dot_t(left, right):
        return lax.dot_general(left, right, (((1,), (1,)), ((), ())), preferred_element_type=F32)

    def forward(d, total):
        other = i - d
        c_in(other).wait_recv()
        return total + dot_t(part_c[other], inv_block(other))

    forward_t = lax.fori_loop(1, i + 1, forward, dot_t(part_c[i], inv_block(i))).astype(BF16)

    def e_copy(chip):
        return remote(send_e.at[chip], recv_e.at[i], e_send.at[chip], e_recv.at[i], 2 * chip + home, j)

    def e_in(other):
        return remote(send_e.at[0], recv_e.at[other], e_send.at[0], e_recv.at[other], other, j)

    @functools.partial(each, 0, z + 1)
    def _(chip):
        left = jnp.dot(forward_t, inv_block(2 * chip), preferred_element_type=F32)
        right = jnp.dot(forward_t, inv_block(2 * chip + 1), preferred_element_type=F32)
        mine = jnp.logical_and(chip == z, core == home)

        @pl.when(mine)
        def _():
            own_e[:, :SHARE] = left
            own_e[:, SHARE:] = right

        @pl.when(jnp.logical_not(mine))
        def _():
            send_e[chip, :, :SHARE] = left.astype(BF16)
            send_e[chip, :, SHARE:] = right.astype(BF16)
            e_copy(chip).start()

    def pair_copy():
        return remote(
            sol_out.at[1 - core], sol_out.at[1 - core], pair_send, pair_recv, mate, j
        )

    def pair_in():
        return remote(sol_out.at[core], sol_out.at[core], pair_send, pair_recv, mate, j)

    out_last = pltpu.make_async_copy(sol_out.at[core], last_hbm, sem_out.at[0])

    my_chip = lax.div(j, 4)
    my_set = lax.rem(j + my_chip, 2)

    def s_copy(other):
        spot = sol_t.at[my_set, my_chip]
        return remote(spot, spot, s_send, s_recv.at[my_set, my_chip], i, other)

    def s_in(side, chip):
        spot = sol_t.at[side, chip]
        return remote(
            spot, spot, s_send, s_recv.at[side, chip], i, lax.rem(j + 1, COLS)
        )

    @pl.when(core == home)
    def _():
        own = own_e[...]

        def add_one(other, total):
            e_in(other).wait_recv()
            return total + recv_e[other].astype(F32)

        own = lax.fori_loop(2 * z, i, add_one, own)
        own = lax.fori_loop(i + 1, ROWS, add_one, own)
        sol_t[my_set, my_chip] = own.astype(BF16)

        @functools.partial(each, 1, COLS)
        def _(d):
            s_copy(lax.rem(j + d, COLS)).start()

        sol_out[0] = own[:, :SHARE]
        sol_out[1] = own[:, SHARE:]
        pair_copy().start()

    @pl.when(core != home)
    def _():
        pair_in().wait_recv()

    out_last.start()

    def solved(side):
        @functools.partial(each, 0, RING)
        def _(chip):
            @pl.when((core != home) | (my_set != side) | (my_chip != chip))
            def _():
                s_in(side, chip).wait_recv()

    def half_copy(t, up):
        n = lax.rem(t, SLOTS)
        return remote(
            half_out.at[n, up], half_in.at[n, up], half_send.at[n], half_recv.at[n],
            row_up if up else row_dn, j,
        )

    def half_both(t):
        n = lax.rem(t, SLOTS)
        return remote(half_out.at[n], half_in.at[n], half_send.at[n], half_recv.at[n], row_up, j)

    def full_copy(t, up):
        n = lax.rem(t, SLOTS)
        return remote(
            full_out.at[n, up], full_in.at[n, up], full_send.at[n], full_recv.at[n],
            row_up if up else row_dn, j,
        )

    def full_both(t):
        n = lax.rem(t, SLOTS)
        return remote(full_out.at[n], full_in.at[n], full_send.at[n], full_recv.at[n], row_up, j)

    def side_of(t):
        late = lax.rem(lax.max(t - 2 * AHEAD, 0), 2)
        return jnp.where(t < 2 * AHEAD, lax.div(t, AHEAD), late)

    def spot_of(t):
        late = AHEAD + lax.div(lax.max(t - 2 * AHEAD, 0), 2)
        return jnp.where(t < 2 * AHEAD, lax.rem(t, AHEAD), late)

    def round_of(spot):
        return lax.rem(spot + ROUNDS - 1, ROUNDS)

    def sides_of(side):
        return pl.ds(pl.multiple_of(side * WIDE, WIDE), WIDE)

    def rows_of(chip):
        return pl.ds(pl.multiple_of(chip * WIDE, WIDE), WIDE)

    def swapped(t):
        spot = spot_of(t)

        @pl.when(spot == 0)
        def _():
            swap_in("last").wait_recv()

        @pl.when((spot > 0) & (lax.rem(spot + GROUP - 1, GROUP) == 0))
        def _():
            swap_in(lax.div(spot - 1, GROUP)).wait_recv()

    def multiply(t, side):
        k = round_of(spot_of(t))
        left = sol_t[side, :, :, :SHARE].reshape(RING * WIDE, SHARE)
        right = sol_t[side, :, :, SHARE:].reshape(RING * WIDE, SHARE)
        return jnp.dot(left, panel[0, k], preferred_element_type=F32) + jnp.dot(
            right, panel[1, k], preferred_element_type=F32
        )

    def multiply_both(t):
        k = round_of(spot_of(t))
        left = sol_t[:, :, :, :SHARE].reshape(2 * RING * WIDE, SHARE)
        right = sol_t[:, :, :, SHARE:].reshape(2 * RING * WIDE, SHARE)
        return jnp.dot(left, panel[0, k], preferred_element_type=F32) + jnp.dot(
            right, panel[1, k], preferred_element_type=F32
        )

    def first(t):
        n = lax.rem(t, SLOTS)

        @pl.when(side_of(t) == 0)
        def _():
            swapped(t)

        @pl.when(t < 2 * AHEAD)
        def _():
            prod[n] = multiply(t, side_of(t))

        @pl.when((t >= 2 * AHEAD) & (side_of(t) == 0))
        def _():
            both = multiply_both(t)
            prod[n] = both[: RING * WIDE]
            prod[lax.rem(t + 1, SLOTS)] = both[RING * WIDE :]

        @pl.when(t >= SLOTS)
        def _():
            half_both(t).wait_send()

        far = prod[n, rows_of(z_far), :].astype(BF16)
        half_out[n, 1] = far[:16]
        half_out[n, 0] = far[16:]
        half_copy(t, 1).start()
        half_copy(t, 0).start()

    def second(t):
        n = lax.rem(t, SLOTS)
        half_both(t).wait_recv()

        @pl.when(t >= SLOTS)
        def _():
            full_both(t).wait_send()

        up = prod[n, rows_of(z_up), :]
        full_out[n, 1, 0:16] = (up[0:16] + half_in[n, 1].astype(F32)).astype(BF16)
        full_out[n, 1, 16:32] = up[16:32].astype(BF16)
        full_copy(t, 1).start()
        dn = prod[n, rows_of(z_dn), :]
        full_out[n, 0, 0:16] = dn[0:16].astype(BF16)
        full_out[n, 0, 16:32] = (dn[16:32] + half_in[n, 0].astype(F32)).astype(BF16)
        full_copy(t, 0).start()

    def third(t):
        side, spot = side_of(t), spot_of(t)
        k = round_of(spot)
        n = lax.rem(t, SLOTS)

        @pl.when(side == 0)
        def _():
            block = known[k, :, pl.ds(pl.multiple_of(z * 128, 128), 128)]
            turn[...] = block.astype(F32).T
            begin[spot] = turn[pl.ds(pl.multiple_of(core * OWN, OWN), OWN), :]

        full_both(t).wait_recv()
        half = lax.rem(side + z, 2)
        sides = sides_of(half)
        terms = prod[n, rows_of(z), :] + full_in[n, 1].astype(F32) + full_in[n, 0].astype(F32)
        done = begin[spot, sides, :] - terms
        for part in range(2):
            where = half * (WIDE * 2 * ROUNDS) + 2 * k + part
            upd[pl.ds(where, WIDE, stride=2 * ROUNDS), :] = done[:, part * 128 : part * 128 + 128]

        @pl.when(spot == 0)
        def _():
            prior[sides, :] = done.astype(BF16)

    def step(t):
        @pl.when(t < STEPS)
        def _():
            first(t)

        @pl.when(jnp.logical_and(t >= LAG_ADD, t < STEPS + LAG_ADD))
        def _():
            second(t - LAG_ADD)

        @pl.when(t >= LAG_END)
        def _():
            third(t - LAG_END)

    solved(0)
    each(0, AHEAD, step)
    solved(1)
    each(AHEAD, AHEAD + LAG_END + 1, step)

    def m_copy(other):
        return remote(send_m.at[other], recv_m.at[j], m_send.at[other], m_recv.at[j], i, other)

    def m_in(other):
        return remote(send_m.at[other], recv_m.at[other], m_send.at[other], m_recv.at[other], i, other)

    prev_load.wait()

    def prev_block(b):
        return prev[:, pl.ds(pl.multiple_of(b * BLOCK, BLOCK), BLOCK)]

    own_m[...] = jnp.dot(prior[...], prev_block(j), preferred_element_type=F32)

    @functools.partial(each, 0, j)
    def _(b):
        send_m[b] = jnp.dot(prior[...], prev_block(b), preferred_element_type=F32).astype(BF16)
        m_copy(b).start()

    each(AHEAD + LAG_END + 1, STEPS + LAG_END, step)

    out_upd = pltpu.make_async_copy(upd, upd_hbm, sem_upd)
    out_upd.start()

    def add_m(other, total):
        m_in(other).wait_recv()
        return total + recv_m[other].astype(F32)

    prev_out[...] = lax.fori_loop(j + 1, COLS, add_m, own_m[...])
    out_prev = pltpu.make_async_copy(prev_out, sol_prev_hbm, sem_out.at[1])
    out_prev.start()

    b_all(0).wait_send()
    b_all(1).wait_send()
    swap_all().wait_send()

    @functools.partial(each, 0, ROWS - 1 - i)
    def _(d):
        c_copy(ROWS - 1 - d).wait_send()

    @functools.partial(each, 0, z + 1)
    def _(chip):
        @pl.when(jnp.logical_not(jnp.logical_and(chip == z, core == home)))
        def _():
            e_copy(chip).wait_send()

    @pl.when(core == home)
    def _():
        pair_copy().wait_send()

        @functools.partial(each, 1, COLS)
        def _(d):
            s_copy(lax.rem(j + d, COLS)).wait_send()

    @functools.partial(each, 0, j)
    def _(b):
        m_copy(b).wait_send()

    @functools.partial(each, STEPS - SLOTS, STEPS)
    def _(t):
        half_both(t).wait_send()
        full_both(t).wait_send()

    out_upd.wait()
    out_last.wait()
    out_prev.wait()


def hand_over(upd_in, last_in, prev_in, upd_out, last_out, prev_out, upd, last, prev, sems):
    def piece(ref, n):
        rows = ref.shape[0] // PIECES
        return ref.at[pl.ds(n * rows, rows)]

    moves = [(last_in, last, last_out), (prev_in, prev, prev_out)]
    moves += [(piece(upd_in, n), piece(upd, n), piece(upd_out, n)) for n in range(PIECES)]
    loads = [pltpu.make_async_copy(a, b, sems.at[0, n]) for n, (a, b, _) in enumerate(moves)]
    stores = [pltpu.make_async_copy(b, c, sems.at[1, n]) for n, (_, b, c) in enumerate(moves)]
    for load in loads:
        load.start()
    for load, store in zip(loads, stores):
        load.wait()
        store.start()
    for store in stores:
        store.wait()


def scratch():
    dma = pltpu.SemaphoreType.DMA
    return [
        pltpu.VMEM((2, ROUNDS, SHARE, BLOCK), BF16),
        pltpu.VMEM((ROUNDS, BLOCK, SIDES), BF16),
        pltpu.VMEM((WIDE, SHARE), F32),
        pltpu.VMEM((SHARE, ROWS * SHARE), BF16),
        pltpu.VMEM((BLOCK, COLS * BLOCK), BF16),
        pltpu.VMEM((256, SIDES), F32),
        pltpu.VMEM((2, COLS, WIDE, 256), BF16),
        pltpu.VMEM((2, COLS, WIDE, 256), BF16),
        pltpu.VMEM((ROWS, WIDE, SHARE), BF16),
        pltpu.VMEM((RING, WIDE, 2 * SHARE), BF16),
        pltpu.VMEM((ROWS, WIDE, 2 * SHARE), BF16),
        pltpu.VMEM((WIDE, 2 * SHARE), F32),
        pltpu.VMEM((2, WIDE, SHARE), F32),
        pltpu.VMEM((2, RING, WIDE, 2 * SHARE), BF16),
        pltpu.VMEM((SLOTS, RING * WIDE, BLOCK), F32),
        pltpu.VMEM((SLOTS, 2, WIDE // 2, BLOCK), BF16),
        pltpu.VMEM((SLOTS, 2, WIDE // 2, BLOCK), BF16),
        pltpu.VMEM((SLOTS, 2, WIDE, BLOCK), BF16),
        pltpu.VMEM((SLOTS, 2, WIDE, BLOCK), BF16),
        pltpu.VMEM((128, BLOCK), F32),
        pltpu.VMEM((ROUNDS, OWN, BLOCK), F32),
        pltpu.VMEM((OWN * ROUNDS * 2, 128), F32),
        pltpu.VMEM((OWN, BLOCK), BF16),
        pltpu.VMEM((OWN, BLOCK), F32),
        pltpu.VMEM((COLS, OWN, BLOCK), BF16),
        pltpu.VMEM((COLS, OWN, BLOCK), BF16),
        pltpu.VMEM((OWN, BLOCK), F32),
        dma((2, GROUPS + 1)),
        dma((GROUPS + 1,)),
        dma(()),
        dma(()),
        dma(()),
        dma((2,)),
        dma(()),
        dma((GROUPS + 1,)),
        dma(()),
        dma((2,)),
        dma((ROWS,)),
        dma((ROWS,)),
        dma((RING,)),
        dma((ROWS,)),
        dma(()),
        dma(()),
        dma(()),
        dma((2, RING)),
        dma((SLOTS,)),
        dma((SLOTS,)),
        dma((SLOTS,)),
        dma((SLOTS,)),
        dma((COLS,)),
        dma((COLS,)),
        dma(()),
    ]


def per_device(factor_panel, solved_prev, rhs_last, inv_last, inv_prev):
    panel = factor_panel.transpose(1, 2, 0, 3).reshape(ROUNDS, SHARE, BLOCK)
    known = solved_prev.reshape(ROUNDS, BLOCK, SIDES)
    anywhere = pl.BlockSpec(memory_space=pl.ANY)
    out_shape = [
        jax.ShapeDtypeStruct((OWN * ROUNDS * 2, 128), F32),
        jax.ShapeDtypeStruct((WIDE, SHARE), F32),
        jax.ShapeDtypeStruct((OWN, BLOCK), F32),
    ]
    results = pl.pallas_call(
        kernel,
        out_shape=out_shape,
        in_specs=[anywhere] * 5,
        out_specs=[anywhere] * 3,
        scratch_shapes=scratch(),
        compiler_params=pltpu.CompilerParams(
            collective_id=0, has_side_effects=True, vmem_limit_bytes=60 * 1024 * 1024
        ),
        cost_estimate=pl.CostEstimate(
            flops=9 * 10**9, bytes_accessed=21 * 10**6, transcendentals=0
        ),
    )(panel, known, rhs_last.T, inv_last, inv_prev.reshape(BLOCK, COLS * BLOCK))
    updated, last_t, prev_t = pl.pallas_call(
        hand_over,
        out_shape=out_shape,
        in_specs=[anywhere] * 3,
        out_specs=[anywhere] * 3,
        scratch_shapes=[pltpu.VMEM(shape.shape, shape.dtype) for shape in out_shape]
        + [pltpu.SemaphoreType.DMA((2, PIECES + 2))],
        compiler_params=pltpu.CompilerParams(vmem_limit_bytes=60 * 1024 * 1024),
    )(*results)
    return updated.reshape(OWN, ROUNDS, 1, BLOCK), last_t.T, prev_t.T


def solution(mesh):
    in_specs = (
        P("row", None, "col", None),
        P(None, "col", None, None),
        P("row", "col"),
        P("row", None),
        P(None, "col", None, None),
    )
    out_specs = (P("row", None, "col", None), P("row", "col"), P("col", "row"))
    return jax.shard_map(
        per_device, mesh=mesh, in_specs=in_specs, out_specs=out_specs, check_vma=False
    )
```

```python
import functools

import jax
import jax.numpy as jnp
from jax import lax
from jax.experimental import pallas as pl
from jax.experimental.pallas import tpu as pltpu
from jax.sharding import PartitionSpec as P

ROWS = 8
COLS = 16
RING = 4
ROUNDS = 31
SIDES = 512
SHARE = 512
BLOCK = 256
WIDE = 32
OWN = 64
GROUP = 6
STEPS = 2 * ROUNDS
AHEAD = 3
LAG_ADD = 10
LAG_END = 20
SLOTS = LAG_END + 2
PIECES = 4
GROUPS = 5
F32 = jnp.float32
BF16 = jnp.bfloat16


def remote(src, dst, send_sem, recv_sem, row, col):
    return pltpu.make_async_remote_copy(
        src_ref=src,
        dst_ref=dst,
        send_sem=send_sem,
        recv_sem=recv_sem,
        device_id=(row, col),
        device_id_type=pl.DeviceIdType.MESH,
    )


def each(start, stop, body):
    def step(index, carry):
        body(index)
        return carry

    lax.fori_loop(start, stop, step, 0)


def kernel(
    panel_hbm, known_hbm, rhs_hbm, inv_hbm, prev_hbm,
    upd_hbm, last_hbm, sol_prev_hbm,
    panel, known, rhs, inv, prev,
    acc, send_b, recv_b, part_c, send_e, recv_e, own_e, sol_out, sol_t,
    prod, half_out, half_in, full_out, full_in,
    turn, begin, upd, prior, own_m, send_m, recv_m, prev_out,
    sem_panel, sem_known, sem_rhs, sem_inv, sem_prev, sem_out,
    swap_send, swap_recv, b_send, b_recv, c_send, c_recv, e_send, e_recv,
    pair_send, pair_recv, s_send, s_recv,
    half_send, half_recv, full_send, full_recv, m_send, m_recv, sem_upd,
):
    i = lax.axis_index("row")
    j = lax.axis_index("col")
    z = lax.div(i, 2)
    core = lax.rem(i, 2)
    mate = i + 1 - 2 * core
    z_up = lax.rem(z + 1, RING)
    z_dn = lax.rem(z + 3, RING)
    z_far = lax.rem(z + 2, RING)
    row_up = 2 * z_up + core
    row_dn = 2 * z_dn + core
    home = lax.rem(lax.div(j, 2), 2)

    def span(g):
        return pl.ds((ROUNDS - 1) if isinstance(g, str) else g * GROUP, 1 if isinstance(g, str) else GROUP)

    def sem_of(g):
        return GROUPS if isinstance(g, str) else g

    def panel_load(h, g):
        rows = pl.ds(h * 256, 256)
        return pltpu.make_async_copy(
            panel_hbm.at[span(g), rows],
            panel.at[core, span(g), rows],
            sem_panel.at[h, sem_of(g)],
        )

    def known_load(g):
        return pltpu.make_async_copy(
            known_hbm.at[span(g)], known.at[span(g)], sem_known.at[sem_of(g)]
        )

    inv_load = pltpu.make_async_copy(inv_hbm, inv, sem_inv)
    prev_load = pltpu.make_async_copy(prev_hbm, prev, sem_prev)
    rhs_load = pltpu.make_async_copy(rhs_hbm, rhs, sem_rhs)

    panel_load(0, "last").start()
    known_load("last").start()

    @functools.partial(each, 0, GROUPS)
    def _(g):
        panel_load(0, g).start()
        known_load(g).start()

    barrier = pltpu.get_barrier_semaphore()

    @functools.partial(each, 1, COLS)
    def _(d):
        pl.semaphore_signal(
            barrier, inc=1, device_id=(i, lax.rem(j + d, COLS)), device_id_type=pl.DeviceIdType.MESH
        )

    @functools.partial(each, 1, ROWS)
    def _(d):
        pl.semaphore_signal(
            barrier, inc=1, device_id=(lax.rem(i + d, ROWS), j), device_id_type=pl.DeviceIdType.MESH
        )

    panel_load(1, "last").start()

    @functools.partial(each, 0, GROUPS)
    def _(g):
        panel_load(1, g).start()

    rhs_load.start()

    def swap(h, g):
        spot = panel.at[core, span(g), pl.ds(h * 256, 256)]
        return remote(spot, spot, swap_send, swap_recv.at[sem_of(g)], mate, j)

    def swap_in(g):
        spot = panel.at[1 - core, span(g)]
        return remote(spot, spot, swap_send, swap_recv.at[sem_of(g)], mate, j)

    def swap_all():
        return remote(panel.at[core], panel.at[core], swap_send, swap_recv.at[0], mate, j)

    def b_copy(h, other):
        return remote(
            send_b.at[h, other], recv_b.at[h, j], b_send, b_recv.at[h], i, other
        )

    def b_all(h):
        rest = pl.ds(0, COLS - 1)
        return remote(
            send_b.at[h, rest], recv_b.at[h, rest], b_send, b_recv.at[h], i, lax.rem(j + 1, COLS)
        )

    for h in range(2):
        rows = pl.ds(h * 256, 256)

        def arrive(g):
            panel_load(h, g).wait()
            if h == 0:
                known_load(g).wait()
            else:
                swap(1, g).start()

        def product(k):
            return jnp.dot(panel[core, k, rows], known[k], preferred_element_type=F32)

        arrive("last")
        acc[...] = product(ROUNDS - 1)

        @functools.partial(each, 0, GROUPS)
        def _(g):
            arrive(g)
            total = product(GROUP * g)
            for u in range(1, GROUP):
                total = total + product(GROUP * g + u)
            acc[...] += total

        for g in range(4):
            flipped = acc[:, g * 128 : g * 128 + 128].T.astype(BF16)
            for u in range(4):
                send_b[h, 4 * g + u] = flipped[u * WIDE : (u + 1) * WIDE]

        if h == 0:
            pl.semaphore_wait(barrier, COLS - 1 + ROWS - 1)

        for odd in range(2):

            @functools.partial(each, 0, COLS // 2)
            def _(half):
                x = lax.rem(lax.div(j, 4) + lax.div(half, 2), 4)
                y = lax.rem(lax.rem(j, 4) + 2 * lax.rem(half, 2), 4)
                other = 4 * x + y + lax.rem(x + y + odd, 2) * (1 - 2 * lax.rem(y, 2))

                @pl.when(other != j)
                def _():
                    b_copy(h, other).start()

        if h == 0:
            swap(0, "last").start()

            @functools.partial(each, 0, GROUPS)
            def _(g):
                swap(0, g).start()

            inv_load.start()
            prev_load.start()

    rhs_load.wait()

    for h in range(2):
        rows = pl.ds(h * 256, 256)

        def subtract(d, total):
            other = lax.rem(j + d, COLS)
            return total - recv_b[h, other].astype(F32)

        b_all(h).wait_recv()
        residue = lax.fori_loop(1, COLS, subtract, rhs[:, rows] - send_b[h, j].astype(F32))
        part_c[i, :, rows] = residue.astype(BF16)

    def c_copy(other):
        return remote(part_c.at[i], part_c.at[i], c_send.at[other], c_recv.at[i], other, j)

    def c_in(other):
        return remote(part_c.at[other], part_c.at[other], c_send.at[other], c_recv.at[other], other, j)

    @functools.partial(each, 0, ROWS - 1 - i)
    def _(d):
        c_copy(ROWS - 1 - d).start()

    inv_load.wait()

    def inv_block(b):
        return inv[:, pl.ds(pl.multiple_of(b * SHARE, SHARE), SHARE)]

    def dot_t(left, right):
        return lax.dot_general(left, right, (((1,), (1,)), ((), ())), preferred_element_type=F32)

    def forward(d, total):
        other = i - d
        c_in(other).wait_recv()
        return total + dot_t(part_c[other], inv_block(other))

    forward_t = lax.fori_loop(1, i + 1, forward, dot_t(part_c[i], inv_block(i))).astype(BF16)

    def e_copy(chip):
        return remote(send_e.at[chip], recv_e.at[i], e_send.at[chip], e_recv.at[i], 2 * chip + home, j)

    def e_in(other):
        return remote(send_e.at[0], recv_e.at[other], e_send.at[0], e_recv.at[other], other, j)

    @functools.partial(each, 0, z + 1)
    def _(chip):
        left = jnp.dot(forward_t, inv_block(2 * chip), preferred_element_type=F32)
        right = jnp.dot(forward_t, inv_block(2 * chip + 1), preferred_element_type=F32)
        mine = jnp.logical_and(chip == z, core == home)

        @pl.when(mine)
        def _():
            own_e[:, :SHARE] = left
            own_e[:, SHARE:] = right

        @pl.when(jnp.logical_not(mine))
        def _():
            send_e[chip, :, :SHARE] = left.astype(BF16)
            send_e[chip, :, SHARE:] = right.astype(BF16)
            e_copy(chip).start()

    def pair_copy():
        return remote(
            sol_out.at[1 - core], sol_out.at[1 - core], pair_send, pair_recv, mate, j
        )

    def pair_in():
        return remote(sol_out.at[core], sol_out.at[core], pair_send, pair_recv, mate, j)

    out_last = pltpu.make_async_copy(sol_out.at[core], last_hbm, sem_out.at[0])

    my_chip = lax.div(j, 4)
    my_set = lax.rem(j + my_chip, 2)

    def s_copy(other):
        spot = sol_t.at[my_set, my_chip]
        return remote(spot, spot, s_send, s_recv.at[my_set, my_chip], i, other)

    def s_in(side, chip):
        spot = sol_t.at[side, chip]
        return remote(
            spot, spot, s_send, s_recv.at[side, chip], i, lax.rem(j + 1, COLS)
        )

    @pl.when(core == home)
    def _():
        own = own_e[...]

        def add_one(other, total):
            e_in(other).wait_recv()
            return total + recv_e[other].astype(F32)

        own = lax.fori_loop(2 * z, i, add_one, own)
        own = lax.fori_loop(i + 1, ROWS, add_one, own)
        sol_t[my_set, my_chip] = own.astype(BF16)

        @functools.partial(each, 0, COLS)
        def _(d):
            x = lax.rem(my_chip + lax.rem(lax.div(d, 2), 4), 4)
            y = 2 * lax.rem(1 + home + lax.div(d, 8), 2) + lax.rem(d, 2)
            other = 4 * x + y

            @pl.when(other != j)
            def _():
                s_copy(other).start()

        sol_out[0] = own[:, :SHARE]
        sol_out[1] = own[:, SHARE:]
        pair_copy().start()


    def solved(side):
        @functools.partial(each, 0, RING)
        def _(chip):
            @pl.when((core != home) | (my_set != side) | (my_chip != chip))
            def _():
                s_in(side, chip).wait_recv()

    def half_copy(t, up):
        n = lax.rem(t, SLOTS)
        return remote(
            half_out.at[n, up], half_in.at[n, up], half_send.at[n], half_recv.at[n],
            row_up if up else row_dn, j,
        )

    def half_both(t):
        n = lax.rem(t, SLOTS)
        return remote(half_out.at[n], half_in.at[n], half_send.at[n], half_recv.at[n], row_up, j)

    def full_copy(t, up):
        n = lax.rem(t, SLOTS)
        return remote(
            full_out.at[n, up], full_in.at[n, up], full_send.at[n], full_recv.at[n],
            row_up if up else row_dn, j,
        )

    def full_both(t):
        n = lax.rem(t, SLOTS)
        return remote(full_out.at[n], full_in.at[n], full_send.at[n], full_recv.at[n], row_up, j)

    def side_of(t):
        late = lax.rem(lax.max(t - 2 * AHEAD, 0), 2)
        return jnp.where(t < 2 * AHEAD, lax.div(t, AHEAD), late)

    def spot_of(t):
        late = AHEAD + lax.div(lax.max(t - 2 * AHEAD, 0), 2)
        return jnp.where(t < 2 * AHEAD, lax.rem(t, AHEAD), late)

    def round_of(spot):
        return lax.rem(spot + ROUNDS - 1, ROUNDS)

    def sides_of(side):
        return pl.ds(pl.multiple_of(side * WIDE, WIDE), WIDE)

    def upd_copy(t):
        sides = sides_of(lax.rem(side_of(t) + z, 2))
        k = round_of(spot_of(t))
        return pltpu.make_async_copy(upd.at[k, sides], upd_hbm.at[k, sides], sem_upd)

    def rows_of(chip):
        return pl.ds(pl.multiple_of(chip * WIDE, WIDE), WIDE)

    def swapped(t):
        spot = spot_of(t)

        @pl.when(spot == 0)
        def _():
            swap_in("last").wait_recv()

        @pl.when((spot > 0) & (lax.rem(spot + GROUP - 1, GROUP) == 0))
        def _():
            swap_in(lax.div(spot - 1, GROUP)).wait_recv()

    def multiply(t, side):
        k = round_of(spot_of(t))
        left = sol_t[side, :, :, :SHARE].reshape(RING * WIDE, SHARE)
        right = sol_t[side, :, :, SHARE:].reshape(RING * WIDE, SHARE)
        return jnp.dot(left, panel[0, k], preferred_element_type=F32) + jnp.dot(
            right, panel[1, k], preferred_element_type=F32
        )

    def multiply_both(t):
        k = round_of(spot_of(t))
        left = sol_t[:, :, :, :SHARE].reshape(2 * RING * WIDE, SHARE)
        right = sol_t[:, :, :, SHARE:].reshape(2 * RING * WIDE, SHARE)
        return jnp.dot(left, panel[0, k], preferred_element_type=F32) + jnp.dot(
            right, panel[1, k], preferred_element_type=F32
        )

    def first(t):
        n = lax.rem(t, SLOTS)

        @pl.when(side_of(t) == 0)
        def _():
            swapped(t)

        @pl.when(t < 2 * AHEAD)
        def _():
            prod[n] = multiply(t, side_of(t))

        @pl.when((t >= 2 * AHEAD) & (side_of(t) == 0))
        def _():
            both = multiply_both(t)
            prod[n] = both[: RING * WIDE]
            prod[lax.rem(t + 1, SLOTS)] = both[RING * WIDE :]

        @pl.when(t >= SLOTS)
        def _():
            half_both(t).wait_send()

        far = prod[n, rows_of(z_far), :].astype(BF16)
        half_out[n, 1] = far[:16]
        half_out[n, 0] = far[16:]
        half_copy(t, 1).start()
        half_copy(t, 0).start()

    def second(t):
        n = lax.rem(t, SLOTS)
        half_both(t).wait_recv()

        @pl.when(t >= SLOTS)
        def _():
            full_both(t).wait_send()

        up = prod[n, rows_of(z_up), :]
        full_out[n, 1, 0:16] = (up[0:16] + half_in[n, 1].astype(F32)).astype(BF16)
        full_out[n, 1, 16:32] = up[16:32].astype(BF16)
        full_copy(t, 1).start()
        dn = prod[n, rows_of(z_dn), :]
        full_out[n, 0, 0:16] = dn[0:16].astype(BF16)
        full_out[n, 0, 16:32] = (dn[16:32] + half_in[n, 0].astype(F32)).astype(BF16)
        full_copy(t, 0).start()

    def third(t):
        side, spot = side_of(t), spot_of(t)
        k = round_of(spot)
        n = lax.rem(t, SLOTS)

        full_both(t).wait_recv()
        half = lax.rem(side + z, 2)
        sides = sides_of(half)
        terms = prod[n, rows_of(z), :] + full_in[n, 1].astype(F32) + full_in[n, 0].astype(F32)
        done = begin[k, sides, :] - terms
        upd[k, sides, :] = done

        @pl.when(spot == 0)
        def _():
            prior[sides, :] = done.astype(BF16)

        upd_copy(t).start()

    def step(t):
        @pl.when(t < STEPS)
        def _():
            first(t)

        @pl.when(jnp.logical_and(t >= LAG_ADD, t < STEPS + LAG_ADD))
        def _():
            second(t - LAG_ADD)

        @pl.when(t >= LAG_END)
        def _():
            third(t - LAG_END)

    @functools.partial(each, 0, ROUNDS)
    def _(k):
        block = known[k, :, pl.ds(pl.multiple_of(z * 128, 128), 128)]
        turn[...] = block.astype(F32).T
        begin[k] = turn[pl.ds(pl.multiple_of(core * OWN, OWN), OWN), :]

    solved(0)
    each(0, AHEAD, step)
    solved(1)
    each(AHEAD, AHEAD + LAG_END + 1, step)

    def m_copy(other):
        return remote(send_m.at[other], recv_m.at[j], m_send.at[other], m_recv.at[j], i, other)

    def m_in(other):
        return remote(send_m.at[other], recv_m.at[other], m_send.at[other], m_recv.at[other], i, other)

    prev_load.wait()

    def prev_block(b):
        return prev[:, pl.ds(pl.multiple_of(b * BLOCK, BLOCK), BLOCK)]

    own_m[...] = jnp.dot(prior[...], prev_block(j), preferred_element_type=F32)

    @functools.partial(each, 0, j)
    def _(b):
        send_m[b] = jnp.dot(prior[...], prev_block(b), preferred_element_type=F32).astype(BF16)
        m_copy(b).start()

    each(AHEAD + LAG_END + 1, STEPS + LAG_END, step)

    def add_m(other, total):
        m_in(other).wait_recv()
        return total + recv_m[other].astype(F32)

    prev_out[...] = lax.fori_loop(j + 1, COLS, add_m, own_m[...])
    out_prev = pltpu.make_async_copy(prev_out, sol_prev_hbm, sem_out.at[1])
    out_prev.start()

    @pl.when(core != home)
    def _():
        pair_in().wait_recv()

    out_last.start()

    b_all(0).wait_send()
    b_all(1).wait_send()
    swap_all().wait_send()

    @functools.partial(each, 0, ROWS - 1 - i)
    def _(d):
        c_copy(ROWS - 1 - d).wait_send()

    @functools.partial(each, 0, z + 1)
    def _(chip):
        @pl.when(jnp.logical_not(jnp.logical_and(chip == z, core == home)))
        def _():
            e_copy(chip).wait_send()

    @pl.when(core == home)
    def _():
        pair_copy().wait_send()

        @functools.partial(each, 1, COLS)
        def _(d):
            s_copy(lax.rem(j + d, COLS)).wait_send()

    @functools.partial(each, 0, j)
    def _(b):
        m_copy(b).wait_send()

    @functools.partial(each, STEPS - SLOTS, STEPS)
    def _(t):
        half_both(t).wait_send()
        full_both(t).wait_send()

    pltpu.make_async_copy(upd, upd_hbm, sem_upd).wait()
    out_last.wait()
    out_prev.wait()


def hand_over(upd_in, last_in, prev_in, upd_out, last_out, prev_out, got, upd, last, prev, sems):
    sides = OWN // PIECES
    small = [(last_in, last, last_out), (prev_in, prev, prev_out)]

    def load(n):
        rows = pl.ds(n * sides, sides)
        return pltpu.make_async_copy(upd_in.at[:, rows], got.at[:, rows], sems.at[0, n])

    def store(n):
        rows = pl.ds(n * sides * 2 * ROUNDS, sides * 2 * ROUNDS)
        return pltpu.make_async_copy(upd.at[rows], upd_out.at[rows], sems.at[1, n])

    loads = [load(n) for n in range(PIECES)]
    stores = [store(n) for n in range(PIECES)]
    for n, (start, middle, end) in enumerate(small):
        loads.append(pltpu.make_async_copy(start, middle, sems.at[0, PIECES + n]))
        stores.append(pltpu.make_async_copy(middle, end, sems.at[1, PIECES + n]))
    for copy in loads:
        copy.start()
    for n, copy in enumerate(loads):
        copy.wait()
        if n < PIECES:
            for k in range(ROUNDS):
                block = got[k, n * sides : (n + 1) * sides, :]
                for part in range(2):
                    where = n * sides * 2 * ROUNDS + 2 * k + part
                    upd[pl.ds(where, sides, stride=2 * ROUNDS), :] = block[
                        :, part * 128 : part * 128 + 128
                    ]
        stores[n].start()
    for copy in stores:
        copy.wait()


def scratch():
    dma = pltpu.SemaphoreType.DMA
    return [
        pltpu.VMEM((2, ROUNDS, SHARE, BLOCK), BF16),
        pltpu.VMEM((ROUNDS, BLOCK, SIDES), BF16),
        pltpu.VMEM((WIDE, SHARE), F32),
        pltpu.VMEM((SHARE, ROWS * SHARE), BF16),
        pltpu.VMEM((BLOCK, COLS * BLOCK), BF16),
        pltpu.VMEM((256, SIDES), F32),
        pltpu.VMEM((2, COLS, WIDE, 256), BF16),
        pltpu.VMEM((2, COLS, WIDE, 256), BF16),
        pltpu.VMEM((ROWS, WIDE, SHARE), BF16),
        pltpu.VMEM((RING, WIDE, 2 * SHARE), BF16),
        pltpu.VMEM((ROWS, WIDE, 2 * SHARE), BF16),
        pltpu.VMEM((WIDE, 2 * SHARE), F32),
        pltpu.VMEM((2, WIDE, SHARE), F32),
        pltpu.VMEM((2, RING, WIDE, 2 * SHARE), BF16),
        pltpu.VMEM((SLOTS, RING * WIDE, BLOCK), F32),
        pltpu.VMEM((SLOTS, 2, WIDE // 2, BLOCK), BF16),
        pltpu.VMEM((SLOTS, 2, WIDE // 2, BLOCK), BF16),
        pltpu.VMEM((SLOTS, 2, WIDE, BLOCK), BF16),
        pltpu.VMEM((SLOTS, 2, WIDE, BLOCK), BF16),
        pltpu.VMEM((128, BLOCK), F32),
        pltpu.VMEM((ROUNDS, OWN, BLOCK), F32),
        pltpu.VMEM((ROUNDS, OWN, BLOCK), F32),
        pltpu.VMEM((OWN, BLOCK), BF16),
        pltpu.VMEM((OWN, BLOCK), F32),
        pltpu.VMEM((COLS, OWN, BLOCK), BF16),
        pltpu.VMEM((COLS, OWN, BLOCK), BF16),
        pltpu.VMEM((OWN, BLOCK), F32),
        dma((2, GROUPS + 1)),
        dma((GROUPS + 1,)),
        dma(()),
        dma(()),
        dma(()),
        dma((2,)),
        dma(()),
        dma((GROUPS + 1,)),
        dma(()),
        dma((2,)),
        dma((ROWS,)),
        dma((ROWS,)),
        dma((RING,)),
        dma((ROWS,)),
        dma(()),
        dma(()),
        dma(()),
        dma((2, RING)),
        dma((SLOTS,)),
        dma((SLOTS,)),
        dma((SLOTS,)),
        dma((SLOTS,)),
        dma((COLS,)),
        dma((COLS,)),
        dma(()),
    ]


def per_device(factor_panel, solved_prev, rhs_last, inv_last, inv_prev):
    panel = factor_panel.transpose(1, 2, 0, 3).reshape(ROUNDS, SHARE, BLOCK)
    known = solved_prev.reshape(ROUNDS, BLOCK, SIDES)
    anywhere = pl.BlockSpec(memory_space=pl.ANY)
    out_shape = [
        jax.ShapeDtypeStruct((OWN * ROUNDS * 2, 128), F32),
        jax.ShapeDtypeStruct((WIDE, SHARE), F32),
        jax.ShapeDtypeStruct((OWN, BLOCK), F32),
    ]
    results = pl.pallas_call(
        kernel,
        out_shape=[jax.ShapeDtypeStruct((ROUNDS, OWN, BLOCK), F32)] + out_shape[1:],
        in_specs=[anywhere] * 5,
        out_specs=[anywhere] * 3,
        scratch_shapes=scratch(),
        compiler_params=pltpu.CompilerParams(
            collective_id=0, has_side_effects=True, vmem_limit_bytes=60 * 1024 * 1024
        ),
        cost_estimate=pl.CostEstimate(
            flops=9 * 10**9, bytes_accessed=21 * 10**6, transcendentals=0
        ),
    )(panel, known, rhs_last.T, inv_last, inv_prev.reshape(BLOCK, COLS * BLOCK))
    updated, last_t, prev_t = pl.pallas_call(
        hand_over,
        out_shape=out_shape,
        in_specs=[anywhere] * 3,
        out_specs=[anywhere] * 3,
        scratch_shapes=[pltpu.VMEM((ROUNDS, OWN, BLOCK), F32)]
        + [pltpu.VMEM(shape.shape, shape.dtype) for shape in out_shape]
        + [pltpu.SemaphoreType.DMA((2, PIECES + 2))],
        compiler_params=pltpu.CompilerParams(vmem_limit_bytes=60 * 1024 * 1024),
    )(*results)
    return updated.reshape(OWN, ROUNDS, 1, BLOCK), last_t.T, prev_t.T


def solution(mesh):
    in_specs = (
        P("row", None, "col", None),
        P(None, "col", None, None),
        P("row", "col"),
        P("row", None),
        P(None, "col", None, None),
    )
    out_specs = (P("row", None, "col", None), P("row", "col"), P("col", "row"))
    return jax.shard_map(
        per_device, mesh=mesh, in_specs=in_specs, out_specs=out_specs, check_vma=False
    )
```

```python
import functools

import jax
import jax.numpy as jnp
from jax import lax
from jax.experimental import pallas as pl
from jax.experimental.pallas import tpu as pltpu
from jax.sharding import PartitionSpec as P

ROWS = 8
COLS = 16
RING = 4
ROUNDS = 31
SIDES = 512
SHARE = 512
BLOCK = 256
WIDE = 32
OWN = 64
GROUP = 6
STEPS = 2 * ROUNDS
AHEAD = 3
LAG_ADD = 10
LAG_END = 20
SLOTS = LAG_END + 2
PIECES = 4
GROUPS = 5
F32 = jnp.float32
BF16 = jnp.bfloat16


def remote(src, dst, send_sem, recv_sem, row, col):
    return pltpu.make_async_remote_copy(
        src_ref=src,
        dst_ref=dst,
        send_sem=send_sem,
        recv_sem=recv_sem,
        device_id=(row, col),
        device_id_type=pl.DeviceIdType.MESH,
    )


def each(start, stop, body):
    def step(index, carry):
        body(index)
        return carry

    lax.fori_loop(start, stop, step, 0)


def kernel(
    panel_hbm, known_hbm, rhs_hbm, inv_hbm, prev_hbm,
    upd_hbm, last_hbm, sol_prev_hbm,
    panel, known, rhs, inv, prev,
    acc, send_b, recv_b, part_c, send_e, recv_e, own_e, sol_out, sol_t,
    prod, half_out, half_in, full_out, full_in,
    turn, begin, upd, prior, own_m, send_m, recv_m, prev_out,
    sem_panel, sem_known, sem_rhs, sem_inv, sem_prev, sem_out,
    swap_send, swap_recv, b_send, b_recv, c_send, c_recv, e_send, e_recv,
    pair_send, pair_recv, s_send, s_recv,
    half_send, half_recv, full_send, full_recv, m_send, m_recv, sem_upd,
):
    i = lax.axis_index("row")
    j = lax.axis_index("col")
    z = lax.div(i, 2)
    core = lax.rem(i, 2)
    mate = i + 1 - 2 * core
    z_up = lax.rem(z + 1, RING)
    z_dn = lax.rem(z + 3, RING)
    z_far = lax.rem(z + 2, RING)
    row_up = 2 * z_up + core
    row_dn = 2 * z_dn + core
    home = lax.rem(lax.div(j, 2), 2)

    def span(g):
        return pl.ds((ROUNDS - 1) if isinstance(g, str) else g * GROUP, 1 if isinstance(g, str) else GROUP)

    def sem_of(g):
        return GROUPS if isinstance(g, str) else g

    def panel_load(h, g):
        rows = pl.ds(h * 256, 256)
        return pltpu.make_async_copy(
            panel_hbm.at[span(g), rows],
            panel.at[core, span(g), rows],
            sem_panel.at[h, sem_of(g)],
        )

    def known_load(g):
        return pltpu.make_async_copy(
            known_hbm.at[span(g)], known.at[span(g)], sem_known.at[sem_of(g)]
        )

    inv_load = pltpu.make_async_copy(inv_hbm, inv, sem_inv)
    prev_load = pltpu.make_async_copy(prev_hbm, prev, sem_prev)
    rhs_load = pltpu.make_async_copy(rhs_hbm, rhs, sem_rhs)

    panel_load(0, "last").start()
    known_load("last").start()

    @functools.partial(each, 0, GROUPS)
    def _(g):
        panel_load(0, g).start()
        known_load(g).start()

    barrier = pltpu.get_barrier_semaphore()

    @functools.partial(each, 1, COLS)
    def _(d):
        pl.semaphore_signal(
            barrier, inc=1, device_id=(i, lax.rem(j + d, COLS)), device_id_type=pl.DeviceIdType.MESH
        )

    @functools.partial(each, 1, ROWS)
    def _(d):
        pl.semaphore_signal(
            barrier, inc=1, device_id=(lax.rem(i + d, ROWS), j), device_id_type=pl.DeviceIdType.MESH
        )

    panel_load(1, "last").start()

    @functools.partial(each, 0, GROUPS)
    def _(g):
        panel_load(1, g).start()

    rhs_load.start()

    def swap(h, g):
        spot = panel.at[core, span(g), pl.ds(h * 256, 256)]
        return remote(spot, spot, swap_send, swap_recv.at[sem_of(g)], mate, j)

    def swap_in(g):
        spot = panel.at[1 - core, span(g)]
        return remote(spot, spot, swap_send, swap_recv.at[sem_of(g)], mate, j)

    def swap_all():
        return remote(panel.at[core], panel.at[core], swap_send, swap_recv.at[0], mate, j)

    def b_copy(h, other):
        return remote(
            send_b.at[h, other], recv_b.at[h, j], b_send, b_recv.at[h], i, other
        )

    def b_all(h):
        rest = pl.ds(0, COLS - 1)
        return remote(
            send_b.at[h, rest], recv_b.at[h, rest], b_send, b_recv.at[h], i, lax.rem(j + 1, COLS)
        )

    for h in range(2):
        rows = pl.ds(h * 256, 256)

        def arrive(g):
            panel_load(h, g).wait()
            if h == 0:
                known_load(g).wait()
            else:
                swap(1, g).start()

        def product(k):
            return jnp.dot(panel[core, k, rows], known[k], preferred_element_type=F32)

        arrive("last")
        acc[...] = product(ROUNDS - 1)

        @functools.partial(each, 0, GROUPS)
        def _(g):
            arrive(g)
            total = product(GROUP * g)
            for u in range(1, GROUP):
                total = total + product(GROUP * g + u)
            acc[...] += total

        for g in range(4):
            flipped = acc[:, g * 128 : g * 128 + 128].T.astype(BF16)
            for u in range(4):
                send_b[h, 4 * g + u] = flipped[u * WIDE : (u + 1) * WIDE]

        if h == 0:
            pl.semaphore_wait(barrier, COLS - 1 + ROWS - 1)

        for odd in range(2):

            @functools.partial(each, 0, COLS // 2)
            def _(half):
                x = lax.rem(lax.div(j, 4) + lax.div(half, 2), 4)
                y = lax.rem(lax.rem(j, 4) + 2 * lax.rem(half, 2), 4)
                other = 4 * x + y + lax.rem(x + y + odd, 2) * (1 - 2 * lax.rem(y, 2))

                @pl.when(other != j)
                def _():
                    b_copy(h, other).start()

        if h == 0:
            swap(0, "last").start()

            @functools.partial(each, 0, GROUPS)
            def _(g):
                swap(0, g).start()

            inv_load.start()
            prev_load.start()

    rhs_load.wait()

    for h in range(2):
        rows = pl.ds(h * 256, 256)

        def subtract(d, total):
            other = lax.rem(j + d, COLS)
            return total - recv_b[h, other].astype(F32)

        b_all(h).wait_recv()
        residue = lax.fori_loop(1, COLS, subtract, rhs[:, rows] - send_b[h, j].astype(F32))
        part_c[i, :, rows] = residue.astype(BF16)

    def c_copy(other):
        return remote(part_c.at[i], part_c.at[i], c_send.at[other], c_recv.at[i], other, j)

    def c_in(other):
        return remote(part_c.at[other], part_c.at[other], c_send.at[other], c_recv.at[other], other, j)

    @functools.partial(each, 0, ROWS - 1 - i)
    def _(d):
        c_copy(ROWS - 1 - d).start()

    inv_load.wait()

    def inv_block(b):
        return inv[:, pl.ds(pl.multiple_of(b * SHARE, SHARE), SHARE)]

    def dot_t(left, right):
        return lax.dot_general(left, right, (((1,), (1,)), ((), ())), preferred_element_type=F32)

    def forward(d, total):
        other = i - d
        c_in(other).wait_recv()
        return total + dot_t(part_c[other], inv_block(other))

    forward_t = lax.fori_loop(1, i + 1, forward, dot_t(part_c[i], inv_block(i))).astype(BF16)

    def e_copy(chip):
        return remote(send_e.at[chip], recv_e.at[i], e_send.at[chip], e_recv.at[i], 2 * chip + home, j)

    def e_in(other):
        return remote(send_e.at[0], recv_e.at[other], e_send.at[0], e_recv.at[other], other, j)

    @functools.partial(each, 0, z + 1)
    def _(step):
        chip = jnp.where((z == 3) & (step < 2), 1 - step, step)
        left = jnp.dot(forward_t, inv_block(2 * chip), preferred_element_type=F32)
        right = jnp.dot(forward_t, inv_block(2 * chip + 1), preferred_element_type=F32)
        mine = jnp.logical_and(chip == z, core == home)

        @pl.when(mine)
        def _():
            own_e[:, :SHARE] = left
            own_e[:, SHARE:] = right

        @pl.when(jnp.logical_not(mine))
        def _():
            send_e[chip, :, :SHARE] = left.astype(BF16)
            send_e[chip, :, SHARE:] = right.astype(BF16)
            e_copy(chip).start()

    def pair_copy():
        return remote(
            sol_out.at[1 - core], sol_out.at[1 - core], pair_send, pair_recv, mate, j
        )

    def pair_in():
        return remote(sol_out.at[core], sol_out.at[core], pair_send, pair_recv, mate, j)

    out_last = pltpu.make_async_copy(sol_out.at[core], last_hbm, sem_out.at[0])

    my_chip = lax.div(j, 4)
    my_set = lax.rem(j + my_chip, 2)

    def s_copy(other):
        spot = sol_t.at[my_set, my_chip]
        return remote(spot, spot, s_send, s_recv.at[my_set, my_chip], i, other)

    def s_in(side, chip):
        spot = sol_t.at[side, chip]
        return remote(
            spot, spot, s_send, s_recv.at[side, chip], i, lax.rem(j + 1, COLS)
        )

    @pl.when(core == home)
    def _():
        own = own_e[...]

        def add_one(other, total):
            e_in(other).wait_recv()
            return total + recv_e[other].astype(F32)

        own = lax.fori_loop(2 * z, i, add_one, own)
        own = lax.fori_loop(i + 1, ROWS, add_one, own)
        sol_t[my_set, my_chip] = own.astype(BF16)

        @functools.partial(each, 0, COLS)
        def _(d):
            x = lax.rem(my_chip + lax.rem(lax.div(d, 2), 4), 4)
            y = 2 * lax.rem(1 + home + lax.div(d, 8), 2) + lax.rem(d, 2)
            other = 4 * x + y

            @pl.when(other != j)
            def _():
                s_copy(other).start()

        sol_out[0] = own[:, :SHARE]
        sol_out[1] = own[:, SHARE:]
        pair_copy().start()


    def solved(side):
        @functools.partial(each, 0, RING)
        def _(chip):
            @pl.when((core != home) | (my_set != side) | (my_chip != chip))
            def _():
                s_in(side, chip).wait_recv()

    def half_copy(t, up):
        n = lax.rem(t, SLOTS)
        return remote(
            half_out.at[t, up], half_in.at[n, up], half_send, half_recv.at[n],
            row_up if up else row_dn, j,
        )

    def half_both(t):
        n = lax.rem(t, SLOTS)
        return remote(half_out.at[t], half_in.at[n], half_send, half_recv.at[n], row_up, j)

    def full_copy(t, up):
        n = lax.rem(t, SLOTS)
        return remote(
            full_out.at[t, up], full_in.at[n, up], full_send, full_recv.at[n],
            row_up if up else row_dn, j,
        )

    def full_both(t):
        n = lax.rem(t, SLOTS)
        return remote(full_out.at[t], full_in.at[n], full_send, full_recv.at[n], row_up, j)

    def side_of(t):
        late = lax.rem(lax.max(t - 2 * AHEAD, 0), 2)
        return jnp.where(t < 2 * AHEAD, lax.div(t, AHEAD), late)

    def spot_of(t):
        late = AHEAD + lax.div(lax.max(t - 2 * AHEAD, 0), 2)
        return jnp.where(t < 2 * AHEAD, lax.rem(t, AHEAD), late)

    def round_of(spot):
        return lax.rem(spot + ROUNDS - 1, ROUNDS)

    def sides_of(side):
        return pl.ds(pl.multiple_of(side * WIDE, WIDE), WIDE)

    def upd_copy(t):
        sides = sides_of(lax.rem(side_of(t) + z, 2))
        k = round_of(spot_of(t))
        return pltpu.make_async_copy(upd.at[k, sides], upd_hbm.at[k, sides], sem_upd)

    def rows_of(chip):
        return pl.ds(pl.multiple_of(chip * WIDE, WIDE), WIDE)

    def swapped(t):
        spot = spot_of(t)

        @pl.when(spot == 0)
        def _():
            swap_in("last").wait_recv()

        @pl.when((spot > 0) & (lax.rem(spot + GROUP - 1, GROUP) == 0))
        def _():
            swap_in(lax.div(spot - 1, GROUP)).wait_recv()

    def multiply(t, side):
        k = round_of(spot_of(t))
        left = sol_t[side, :, :, :SHARE].reshape(RING * WIDE, SHARE)
        right = sol_t[side, :, :, SHARE:].reshape(RING * WIDE, SHARE)
        return jnp.dot(left, panel[0, k], preferred_element_type=F32) + jnp.dot(
            right, panel[1, k], preferred_element_type=F32
        )

    def multiply_both(t):
        k = round_of(spot_of(t))
        left = sol_t[:, :, :, :SHARE].reshape(2 * RING * WIDE, SHARE)
        right = sol_t[:, :, :, SHARE:].reshape(2 * RING * WIDE, SHARE)
        return jnp.dot(left, panel[0, k], preferred_element_type=F32) + jnp.dot(
            right, panel[1, k], preferred_element_type=F32
        )

    def first(t):
        n = lax.rem(t, SLOTS)

        @pl.when(side_of(t) == 0)
        def _():
            swapped(t)

        @pl.when(t < 2 * AHEAD)
        def _():
            prod[n] = multiply(t, side_of(t))

        @pl.when((t >= 2 * AHEAD) & (side_of(t) == 0))
        def _():
            both = multiply_both(t)
            prod[n] = both[: RING * WIDE]
            prod[lax.rem(t + 1, SLOTS)] = both[RING * WIDE :]

        far = prod[n, rows_of(z_far), :].astype(BF16)
        half_out[t, 1] = far[:16]
        half_out[t, 0] = far[16:]
        half_copy(t, 1).start()
        half_copy(t, 0).start()

    def second(t):
        n = lax.rem(t, SLOTS)
        half_both(t).wait_recv()

        up = prod[n, rows_of(z_up), :]
        full_out[t, 1, 0:16] = (up[0:16] + half_in[n, 1].astype(F32)).astype(BF16)
        full_out[t, 1, 16:32] = up[16:32].astype(BF16)
        full_copy(t, 1).start()
        dn = prod[n, rows_of(z_dn), :]
        full_out[t, 0, 0:16] = dn[0:16].astype(BF16)
        full_out[t, 0, 16:32] = (dn[16:32] + half_in[n, 0].astype(F32)).astype(BF16)
        full_copy(t, 0).start()

    def third(t):
        side, spot = side_of(t), spot_of(t)
        k = round_of(spot)
        n = lax.rem(t, SLOTS)

        full_both(t).wait_recv()
        half = lax.rem(side + z, 2)
        sides = sides_of(half)
        terms = prod[n, rows_of(z), :] + full_in[n, 1].astype(F32) + full_in[n, 0].astype(F32)
        done = begin[k, sides, :] - terms
        upd[k, sides, :] = done

        @pl.when(spot == 0)
        def _():
            prior[sides, :] = done.astype(BF16)

        upd_copy(t).start()

    def step(t):
        @pl.when(t < STEPS)
        def _():
            first(t)

        @pl.when(jnp.logical_and(t >= LAG_ADD, t < STEPS + LAG_ADD))
        def _():
            second(t - LAG_ADD)

        @pl.when(t >= LAG_END)
        def _():
            third(t - LAG_END)

    @functools.partial(each, 0, ROUNDS)
    def _(k):
        block = known[k, :, pl.ds(pl.multiple_of(z * 128, 128), 128)]
        turn[...] = block.astype(F32).T
        begin[k] = turn[pl.ds(pl.multiple_of(core * OWN, OWN), OWN), :]

    solved(0)
    each(0, AHEAD, step)
    solved(1)
    each(AHEAD, AHEAD + LAG_END + 1, step)

    def m_copy(other):
        return remote(send_m.at[other], recv_m.at[j], m_send.at[other], m_recv.at[j], i, other)

    def m_in(other):
        return remote(send_m.at[other], recv_m.at[other], m_send.at[other], m_recv.at[other], i, other)

    prev_load.wait()

    def prev_block(b):
        return prev[:, pl.ds(pl.multiple_of(b * BLOCK, BLOCK), BLOCK)]

    own_m[...] = jnp.dot(prior[...], prev_block(j), preferred_element_type=F32)

    @functools.partial(each, 0, j)
    def _(b):
        send_m[b] = jnp.dot(prior[...], prev_block(b), preferred_element_type=F32).astype(BF16)
        m_copy(b).start()

    each(AHEAD + LAG_END + 1, STEPS + LAG_END, step)

    def add_m(other, total):
        m_in(other).wait_recv()
        return total + recv_m[other].astype(F32)

    prev_out[...] = lax.fori_loop(j + 1, COLS, add_m, own_m[...])
    out_prev = pltpu.make_async_copy(prev_out, sol_prev_hbm, sem_out.at[1])
    out_prev.start()

    @pl.when(core != home)
    def _():
        pair_in().wait_recv()

    out_last.start()

    b_all(0).wait_send()
    b_all(1).wait_send()
    swap_all().wait_send()

    @functools.partial(each, 0, ROWS - 1 - i)
    def _(d):
        c_copy(ROWS - 1 - d).wait_send()

    @functools.partial(each, 0, z + 1)
    def _(chip):
        @pl.when(jnp.logical_not(jnp.logical_and(chip == z, core == home)))
        def _():
            e_copy(chip).wait_send()

    @pl.when(core == home)
    def _():
        pair_copy().wait_send()

        @functools.partial(each, 1, COLS)
        def _(d):
            s_copy(lax.rem(j + d, COLS)).wait_send()

    @functools.partial(each, 0, j)
    def _(b):
        m_copy(b).wait_send()

    remote(half_out, half_out, half_send, half_recv.at[0], row_up, j).wait_send()
    remote(full_out, full_out, full_send, full_recv.at[0], row_up, j).wait_send()

    pltpu.make_async_copy(upd, upd_hbm, sem_upd).wait()
    out_last.wait()
    out_prev.wait()


def hand_over(upd_in, last_in, prev_in, upd_out, last_out, prev_out, got, upd, last, prev, sems):
    sides = OWN // PIECES
    small = [(last_in, last, last_out), (prev_in, prev, prev_out)]

    def load(n):
        rows = pl.ds(n * sides, sides)
        return pltpu.make_async_copy(upd_in.at[:, rows], got.at[:, rows], sems.at[0, n])

    def store(n):
        rows = pl.ds(n * sides * 2 * ROUNDS, sides * 2 * ROUNDS)
        return pltpu.make_async_copy(upd.at[rows], upd_out.at[rows], sems.at[1, n])

    loads = [load(n) for n in range(PIECES)]
    stores = [store(n) for n in range(PIECES)]
    for n, (start, middle, end) in enumerate(small):
        loads.append(pltpu.make_async_copy(start, middle, sems.at[0, PIECES + n]))
        stores.append(pltpu.make_async_copy(middle, end, sems.at[1, PIECES + n]))
    for copy in loads:
        copy.start()
    for n, copy in enumerate(loads):
        copy.wait()
        if n < PIECES:
            for k in range(ROUNDS):
                block = got[k, n * sides : (n + 1) * sides, :]
                for part in range(2):
                    where = n * sides * 2 * ROUNDS + 2 * k + part
                    upd[pl.ds(where, sides, stride=2 * ROUNDS), :] = block[
                        :, part * 128 : part * 128 + 128
                    ]
        stores[n].start()
    for copy in stores:
        copy.wait()


def scratch():
    dma = pltpu.SemaphoreType.DMA
    return [
        pltpu.VMEM((2, ROUNDS, SHARE, BLOCK), BF16),
        pltpu.VMEM((ROUNDS, BLOCK, SIDES), BF16),
        pltpu.VMEM((WIDE, SHARE), F32),
        pltpu.VMEM((SHARE, ROWS * SHARE), BF16),
        pltpu.VMEM((BLOCK, COLS * BLOCK), BF16),
        pltpu.VMEM((256, SIDES), F32),
        pltpu.VMEM((2, COLS, WIDE, 256), BF16),
        pltpu.VMEM((2, COLS, WIDE, 256), BF16),
        pltpu.VMEM((ROWS, WIDE, SHARE), BF16),
        pltpu.VMEM((RING, WIDE, 2 * SHARE), BF16),
        pltpu.VMEM((ROWS, WIDE, 2 * SHARE), BF16),
        pltpu.VMEM((WIDE, 2 * SHARE), F32),
        pltpu.VMEM((2, WIDE, SHARE), F32),
        pltpu.VMEM((2, RING, WIDE, 2 * SHARE), BF16),
        pltpu.VMEM((SLOTS, RING * WIDE, BLOCK), F32),
        pltpu.VMEM((STEPS, 2, WIDE // 2, BLOCK), BF16),
        pltpu.VMEM((SLOTS, 2, WIDE // 2, BLOCK), BF16),
        pltpu.VMEM((STEPS, 2, WIDE, BLOCK), BF16),
        pltpu.VMEM((SLOTS, 2, WIDE, BLOCK), BF16),
        pltpu.VMEM((128, BLOCK), F32),
        pltpu.VMEM((ROUNDS, OWN, BLOCK), F32),
        pltpu.VMEM((ROUNDS, OWN, BLOCK), F32),
        pltpu.VMEM((OWN, BLOCK), BF16),
        pltpu.VMEM((OWN, BLOCK), F32),
        pltpu.VMEM((COLS, OWN, BLOCK), BF16),
        pltpu.VMEM((COLS, OWN, BLOCK), BF16),
        pltpu.VMEM((OWN, BLOCK), F32),
        dma((2, GROUPS + 1)),
        dma((GROUPS + 1,)),
        dma(()),
        dma(()),
        dma(()),
        dma((2,)),
        dma(()),
        dma((GROUPS + 1,)),
        dma(()),
        dma((2,)),
        dma((ROWS,)),
        dma((ROWS,)),
        dma((RING,)),
        dma((ROWS,)),
        dma(()),
        dma(()),
        dma(()),
        dma((2, RING)),
        dma(()),
        dma((SLOTS,)),
        dma(()),
        dma((SLOTS,)),
        dma((COLS,)),
        dma((COLS,)),
        dma(()),
    ]


def per_device(factor_panel, solved_prev, rhs_last, inv_last, inv_prev):
    panel = factor_panel.transpose(1, 2, 0, 3).reshape(ROUNDS, SHARE, BLOCK)
    known = solved_prev.reshape(ROUNDS, BLOCK, SIDES)
    anywhere = pl.BlockSpec(memory_space=pl.ANY)
    out_shape = [
        jax.ShapeDtypeStruct((OWN * ROUNDS * 2, 128), F32),
        jax.ShapeDtypeStruct((WIDE, SHARE), F32),
        jax.ShapeDtypeStruct((OWN, BLOCK), F32),
    ]
    results = pl.pallas_call(
        kernel,
        out_shape=[jax.ShapeDtypeStruct((ROUNDS, OWN, BLOCK), F32)] + out_shape[1:],
        in_specs=[anywhere] * 5,
        out_specs=[anywhere] * 3,
        scratch_shapes=scratch(),
        compiler_params=pltpu.CompilerParams(
            collective_id=0, has_side_effects=True, vmem_limit_bytes=60 * 1024 * 1024
        ),
        cost_estimate=pl.CostEstimate(
            flops=9 * 10**9, bytes_accessed=21 * 10**6, transcendentals=0
        ),
    )(panel, known, rhs_last.T, inv_last, inv_prev.reshape(BLOCK, COLS * BLOCK))
    updated, last_t, prev_t = pl.pallas_call(
        hand_over,
        out_shape=out_shape,
        in_specs=[anywhere] * 3,
        out_specs=[anywhere] * 3,
        scratch_shapes=[pltpu.VMEM((ROUNDS, OWN, BLOCK), F32)]
        + [pltpu.VMEM(shape.shape, shape.dtype) for shape in out_shape]
        + [pltpu.SemaphoreType.DMA((2, PIECES + 2))],
        compiler_params=pltpu.CompilerParams(vmem_limit_bytes=60 * 1024 * 1024),
    )(*results)
    return updated.reshape(OWN, ROUNDS, 1, BLOCK), last_t.T, prev_t.T


def solution(mesh):
    in_specs = (
        P("row", None, "col", None),
        P(None, "col", None, None),
        P("row", "col"),
        P("row", None),
        P(None, "col", None, None),
    )
    out_specs = (P("row", None, "col", None), P("row", "col"), P("col", "row"))
    return jax.shard_map(
        per_device, mesh=mesh, in_specs=in_specs, out_specs=out_specs, check_vma=False
    )
```

```python
import functools

import jax
import jax.numpy as jnp
from jax import lax
from jax.experimental import pallas as pl
from jax.experimental.pallas import tpu as pltpu
from jax.sharding import PartitionSpec as P

ROWS = 8
COLS = 16
RING = 4
ROUNDS = 31
SIDES = 512
SHARE = 512
BLOCK = 256
WIDE = 32
OWN = 64
GROUP = 6
STEPS = 2 * ROUNDS
AHEAD = 3
LAG_ADD = 10
LAG_END = 20
SLOTS = LAG_END + 2
PIECES = 4
GROUPS = 5
F32 = jnp.float32
BF16 = jnp.bfloat16


def remote(src, dst, send_sem, recv_sem, row, col):
    return pltpu.make_async_remote_copy(
        src_ref=src,
        dst_ref=dst,
        send_sem=send_sem,
        recv_sem=recv_sem,
        device_id=(row, col),
        device_id_type=pl.DeviceIdType.MESH,
    )


def each(start, stop, body):
    def step(index, carry):
        body(index)
        return carry

    lax.fori_loop(start, stop, step, 0)


def kernel(
    panel_hbm, known_hbm, rhs_hbm, inv_hbm, prev_hbm,
    upd_hbm, last_hbm, sol_prev_hbm,
    panel, known, rhs, inv, prev,
    acc, send_b, recv_b, part_c, send_e, recv_e, own_e, sol_out, sol_t,
    prod, half_out, half_in, full_out, full_in,
    turn, begin, upd, prior, own_m, send_m, recv_m, prev_out,
    sem_panel, sem_known, sem_rhs, sem_inv, sem_prev, sem_out,
    swap_send, swap_recv, b_send, b_recv, c_send, c_recv, e_send, e_recv,
    pair_send, pair_recv, s_send, s_recv,
    half_send, half_recv, full_send, full_recv, m_send, m_recv, sem_upd,
):
    i = lax.axis_index("row")
    j = lax.axis_index("col")
    z = lax.div(i, 2)
    core = lax.rem(i, 2)
    mate = i + 1 - 2 * core
    z_up = lax.rem(z + 1, RING)
    z_dn = lax.rem(z + 3, RING)
    z_far = lax.rem(z + 2, RING)
    row_up = 2 * z_up + core
    row_dn = 2 * z_dn + core
    home = lax.rem(lax.div(j, 2), 2)

    def span(g):
        return pl.ds((ROUNDS - 1) if isinstance(g, str) else g * GROUP, 1 if isinstance(g, str) else GROUP)

    def sem_of(g):
        return GROUPS if isinstance(g, str) else g

    def panel_load(h, g):
        rows = pl.ds(h * 256, 256)
        return pltpu.make_async_copy(
            panel_hbm.at[span(g), rows],
            panel.at[core, span(g), rows],
            sem_panel.at[h, sem_of(g)],
        )

    def known_load(g):
        return pltpu.make_async_copy(
            known_hbm.at[span(g)], known.at[span(g)], sem_known.at[sem_of(g)]
        )

    inv_load = pltpu.make_async_copy(inv_hbm, inv, sem_inv)
    prev_load = pltpu.make_async_copy(prev_hbm, prev, sem_prev)
    rhs_load = pltpu.make_async_copy(rhs_hbm, rhs, sem_rhs)

    panel_load(0, "last").start()
    known_load("last").start()

    @functools.partial(each, 0, GROUPS)
    def _(g):
        panel_load(0, g).start()
        known_load(g).start()

    barrier = pltpu.get_barrier_semaphore()

    @functools.partial(each, 1, COLS)
    def _(d):
        pl.semaphore_signal(
            barrier, inc=1, device_id=(i, lax.rem(j + d, COLS)), device_id_type=pl.DeviceIdType.MESH
        )

    @functools.partial(each, 1, ROWS)
    def _(d):
        pl.semaphore_signal(
            barrier, inc=1, device_id=(lax.rem(i + d, ROWS), j), device_id_type=pl.DeviceIdType.MESH
        )

    panel_load(1, "last").start()

    @functools.partial(each, 0, GROUPS)
    def _(g):
        panel_load(1, g).start()

    rhs_load.start()

    def swap(h, g):
        spot = panel.at[core, span(g), pl.ds(h * 256, 256)]
        return remote(spot, spot, swap_send, swap_recv.at[sem_of(g)], mate, j)

    def swap_in(g):
        spot = panel.at[1 - core, span(g)]
        return remote(spot, spot, swap_send, swap_recv.at[sem_of(g)], mate, j)

    def swap_all():
        return remote(panel.at[core], panel.at[core], swap_send, swap_recv.at[0], mate, j)

    def b_copy(h, other):
        return remote(
            send_b.at[h, other], recv_b.at[h, j], b_send, b_recv.at[h], i, other
        )

    def b_all(h):
        rest = pl.ds(0, COLS - 1)
        return remote(
            send_b.at[h, rest], recv_b.at[h, rest], b_send, b_recv.at[h], i, lax.rem(j + 1, COLS)
        )

    for h in range(2):
        rows = pl.ds(h * 256, 256)

        def arrive(g):
            panel_load(h, g).wait()
            if h == 0:
                known_load(g).wait()
            else:
                swap(1, g).start()

        def product(k):
            return jnp.dot(panel[core, k, rows], known[k], preferred_element_type=F32)

        arrive("last")
        acc[...] = product(ROUNDS - 1)

        @functools.partial(each, 0, GROUPS)
        def _(g):
            arrive(g)
            total = product(GROUP * g)
            for u in range(1, GROUP):
                total = total + product(GROUP * g + u)
            acc[...] += total

        for g in range(4):
            flipped = acc[:, g * 128 : g * 128 + 128].T.astype(BF16)
            for u in range(4):
                send_b[h, 4 * g + u] = flipped[u * WIDE : (u + 1) * WIDE]

        if h == 0:
            pl.semaphore_wait(barrier, COLS - 1 + ROWS - 1)

        for odd in range(2):

            @functools.partial(each, 0, COLS // 2)
            def _(half):
                x = lax.rem(lax.div(j, 4) + lax.div(half, 2), 4)
                y = lax.rem(lax.rem(j, 4) + 2 * lax.rem(half, 2), 4)
                other = 4 * x + y + lax.rem(x + y + odd, 2) * (1 - 2 * lax.rem(y, 2))

                @pl.when(other != j)
                def _():
                    b_copy(h, other).start()

        if h == 0:
            swap(0, "last").start()

            @functools.partial(each, 0, GROUPS)
            def _(g):
                swap(0, g).start()

            inv_load.start()
            prev_load.start()

    rhs_load.wait()

    for h in range(2):
        rows = pl.ds(h * 256, 256)

        def subtract(d, total):
            other = lax.rem(j + d, COLS)
            return total - recv_b[h, other].astype(F32)

        b_all(h).wait_recv()
        residue = lax.fori_loop(1, COLS, subtract, rhs[:, rows] - send_b[h, j].astype(F32))
        part_c[i, :, rows] = residue.astype(BF16)

    def c_copy(other):
        return remote(part_c.at[i], part_c.at[i], c_send.at[other], c_recv.at[i], other, j)

    def c_in(other):
        return remote(part_c.at[other], part_c.at[other], c_send.at[other], c_recv.at[other], other, j)

    @functools.partial(each, 0, ROWS - 1 - i)
    def _(d):
        c_copy(ROWS - 1 - d).start()

    inv_load.wait()

    def inv_block(b):
        return inv[:, pl.ds(pl.multiple_of(b * SHARE, SHARE), SHARE)]

    def dot_t(left, right):
        return lax.dot_general(left, right, (((1,), (1,)), ((), ())), preferred_element_type=F32)

    def forward(d, total):
        other = i - d
        c_in(other).wait_recv()
        return total + dot_t(part_c[other], inv_block(other))

    forward_t = lax.fori_loop(1, i + 1, forward, dot_t(part_c[i], inv_block(i))).astype(BF16)

    def e_copy(chip):
        return remote(send_e.at[chip], recv_e.at[i], e_send.at[chip], e_recv.at[i], 2 * chip + home, j)

    def e_in(other):
        return remote(send_e.at[0], recv_e.at[other], e_send.at[0], e_recv.at[other], other, j)

    @functools.partial(each, 0, z + 1)
    def _(step):
        chip = jnp.where((z == 3) & (step < 2), 1 - step, step)
        left = jnp.dot(forward_t, inv_block(2 * chip), preferred_element_type=F32)
        right = jnp.dot(forward_t, inv_block(2 * chip + 1), preferred_element_type=F32)
        mine = jnp.logical_and(chip == z, core == home)

        @pl.when(mine)
        def _():
            own_e[:, :SHARE] = left
            own_e[:, SHARE:] = right

        @pl.when(jnp.logical_not(mine))
        def _():
            send_e[chip, :, :SHARE] = left.astype(BF16)
            send_e[chip, :, SHARE:] = right.astype(BF16)
            e_copy(chip).start()

    def pair_copy():
        return remote(
            sol_out.at[1 - core], sol_out.at[1 - core], pair_send, pair_recv, mate, j
        )

    def pair_in():
        return remote(sol_out.at[core], sol_out.at[core], pair_send, pair_recv, mate, j)

    out_last = pltpu.make_async_copy(sol_out.at[core], last_hbm, sem_out.at[0])

    my_chip = lax.div(j, 4)
    my_set = lax.rem(j + my_chip, 2)

    def s_copy(other):
        spot = sol_t.at[my_set, my_chip]
        return remote(spot, spot, s_send, s_recv.at[my_set, my_chip], i, other)

    def s_in(side, chip):
        spot = sol_t.at[side, chip]
        return remote(
            spot, spot, s_send, s_recv.at[side, chip], i, lax.rem(j + 1, COLS)
        )

    @pl.when(core == home)
    def _():
        own = own_e[...]

        def add_one(other, total):
            e_in(other).wait_recv()
            return total + recv_e[other].astype(F32)

        own = lax.fori_loop(2 * z, i, add_one, own)
        own = lax.fori_loop(i + 1, ROWS, add_one, own)
        sol_t[my_set, my_chip] = own.astype(BF16)

        @functools.partial(each, 0, COLS)
        def _(d):
            x = lax.rem(my_chip + lax.rem(lax.div(d, 2), 4), 4)
            y = 2 * lax.rem(1 + home + lax.div(d, 8), 2) + lax.rem(d, 2)
            other = 4 * x + y

            @pl.when(other != j)
            def _():
                s_copy(other).start()

        sol_out[0] = own[:, :SHARE]
        sol_out[1] = own[:, SHARE:]
        pair_copy().start()


    def solved(side):
        @functools.partial(each, 0, RING)
        def _(chip):
            @pl.when((core != home) | (my_set != side) | (my_chip != chip))
            def _():
                s_in(side, chip).wait_recv()

    def half_copy(t, up):
        n = lax.rem(t, SLOTS)
        return remote(
            half_out.at[t, up], half_in.at[n, up], half_send, half_recv.at[n],
            row_up if up else row_dn, j,
        )

    def half_both(t):
        n = lax.rem(t, SLOTS)
        return remote(half_out.at[t], half_in.at[n], half_send, half_recv.at[n], row_up, j)

    def full_copy(t, up):
        n = lax.rem(t, SLOTS)
        return remote(
            full_out.at[t, up], full_in.at[n, up], full_send, full_recv.at[n],
            row_up if up else row_dn, j,
        )

    def full_both(t):
        n = lax.rem(t, SLOTS)
        return remote(full_out.at[t], full_in.at[n], full_send, full_recv.at[n], row_up, j)

    def side_of(t):
        late = lax.rem(lax.max(t - 2 * AHEAD, 0), 2)
        return jnp.where(t < 2 * AHEAD, lax.div(t, AHEAD), late)

    def spot_of(t):
        late = AHEAD + lax.div(lax.max(t - 2 * AHEAD, 0), 2)
        return jnp.where(t < 2 * AHEAD, lax.rem(t, AHEAD), late)

    def round_of(spot):
        return lax.rem(spot + ROUNDS - 1, ROUNDS)

    def sides_of(side):
        return pl.ds(pl.multiple_of(side * WIDE, WIDE), WIDE)

    def upd_copy(t):
        sides = sides_of(lax.rem(side_of(t) + z, 2))
        k = round_of(spot_of(t))
        return pltpu.make_async_copy(upd.at[k, sides], upd_hbm.at[k, sides], sem_upd)

    def rows_of(chip):
        return pl.ds(pl.multiple_of(chip * WIDE, WIDE), WIDE)

    def swapped(t):
        spot = spot_of(t)

        @pl.when(spot == 0)
        def _():
            swap_in("last").wait_recv()

        @pl.when((spot > 0) & (lax.rem(spot + GROUP - 1, GROUP) == 0))
        def _():
            swap_in(lax.div(spot - 1, GROUP)).wait_recv()

    def multiply(t, side):
        k = round_of(spot_of(t))
        left = sol_t[side, :, :, :SHARE].reshape(RING * WIDE, SHARE)
        right = sol_t[side, :, :, SHARE:].reshape(RING * WIDE, SHARE)
        return jnp.dot(left, panel[0, k], preferred_element_type=F32) + jnp.dot(
            right, panel[1, k], preferred_element_type=F32
        )

    def multiply_both(t):
        k = round_of(spot_of(t))
        left = sol_t[:, :, :, :SHARE].reshape(2 * RING * WIDE, SHARE)
        right = sol_t[:, :, :, SHARE:].reshape(2 * RING * WIDE, SHARE)
        return jnp.dot(left, panel[0, k], preferred_element_type=F32) + jnp.dot(
            right, panel[1, k], preferred_element_type=F32
        )

    def first(t):
        n = lax.rem(t, SLOTS)

        @pl.when(side_of(t) == 0)
        def _():
            swapped(t)

        @pl.when(t < 2 * AHEAD)
        def _():
            prod[n] = multiply(t, side_of(t))

        @pl.when((t >= 2 * AHEAD) & (side_of(t) == 0))
        def _():
            both = multiply_both(t)
            prod[n] = both[: RING * WIDE]
            prod[lax.rem(t + 1, SLOTS)] = both[RING * WIDE :]

        far = prod[n, rows_of(z_far), :].astype(BF16)
        half_out[t, 1] = far[:16]
        half_out[t, 0] = far[16:]
        half_copy(t, 1).start()
        half_copy(t, 0).start()

    def second(t):
        n = lax.rem(t, SLOTS)
        half_both(t).wait_recv()

        up = prod[n, rows_of(z_up), :]
        full_out[t, 1, 0:16] = (up[0:16] + half_in[n, 1].astype(F32)).astype(BF16)
        full_out[t, 1, 16:32] = up[16:32].astype(BF16)
        full_copy(t, 1).start()
        dn = prod[n, rows_of(z_dn), :]
        full_out[t, 0, 0:16] = dn[0:16].astype(BF16)
        full_out[t, 0, 16:32] = (dn[16:32] + half_in[n, 0].astype(F32)).astype(BF16)
        full_copy(t, 0).start()

    def third(t):
        side, spot = side_of(t), spot_of(t)
        k = round_of(spot)
        n = lax.rem(t, SLOTS)

        full_both(t).wait_recv()
        half = lax.rem(side + z, 2)
        sides = sides_of(half)
        terms = prod[n, rows_of(z), :] + full_in[n, 1].astype(F32) + full_in[n, 0].astype(F32)
        done = begin[k, sides, :] - terms
        upd[k, sides, :] = done

        @pl.when(spot == 0)
        def _():
            prior[sides, :] = done.astype(BF16)

        upd_copy(t).start()

    def step(t):
        @pl.when(t < STEPS)
        def _():
            first(t)

        @pl.when(jnp.logical_and(t >= LAG_ADD, t < STEPS + LAG_ADD))
        def _():
            second(t - LAG_ADD)

        @pl.when(t >= LAG_END)
        def _():
            third(t - LAG_END)

    @functools.partial(each, 0, ROUNDS)
    def _(k):
        block = known[k, :, pl.ds(pl.multiple_of(z * 128, 128), 128)]
        turn[...] = block.astype(F32).T
        begin[k] = turn[pl.ds(pl.multiple_of(core * OWN, OWN), OWN), :]

    solved(0)
    each(0, AHEAD, step)
    solved(1)
    each(AHEAD, AHEAD + LAG_END + 1, step)

    def m_copy(other):
        return remote(send_m.at[other], recv_m.at[j], m_send.at[other], m_recv.at[j], i, other)

    def m_in(other):
        return remote(send_m.at[other], recv_m.at[other], m_send.at[other], m_recv.at[other], i, other)

    prev_load.wait()

    def prev_block(b):
        return prev[:, pl.ds(pl.multiple_of(b * BLOCK, BLOCK), BLOCK)]

    own_m[...] = jnp.dot(prior[...], prev_block(j), preferred_element_type=F32)

    @functools.partial(each, 0, j)
    def _(b):
        send_m[b] = jnp.dot(prior[...], prev_block(b), preferred_element_type=F32).astype(BF16)
        m_copy(b).start()

    each(AHEAD + LAG_END + 1, STEPS + LAG_END, step)

    def add_m(other, total):
        m_in(other).wait_recv()
        return total + recv_m[other].astype(F32)

    prev_out[...] = lax.fori_loop(j + 1, COLS, add_m, own_m[...])
    out_prev = pltpu.make_async_copy(prev_out, sol_prev_hbm, sem_out.at[1])
    out_prev.start()

    @pl.when(core != home)
    def _():
        pair_in().wait_recv()

    out_last.start()

    b_all(0).wait_send()
    b_all(1).wait_send()
    swap_all().wait_send()

    @functools.partial(each, 0, ROWS - 1 - i)
    def _(d):
        c_copy(ROWS - 1 - d).wait_send()

    @functools.partial(each, 0, z + 1)
    def _(chip):
        @pl.when(jnp.logical_not(jnp.logical_and(chip == z, core == home)))
        def _():
            e_copy(chip).wait_send()

    @pl.when(core == home)
    def _():
        pair_copy().wait_send()

        @functools.partial(each, 1, COLS)
        def _(d):
            s_copy(lax.rem(j + d, COLS)).wait_send()

    @functools.partial(each, 0, j)
    def _(b):
        m_copy(b).wait_send()

    remote(half_out, half_out, half_send, half_recv.at[0], row_up, j).wait_send()
    remote(full_out, full_out, full_send, full_recv.at[0], row_up, j).wait_send()

    pltpu.make_async_copy(upd, upd_hbm, sem_upd).wait()
    out_last.wait()
    out_prev.wait()


def hand_over(upd_in, last_in, prev_in, upd_out, last_out, prev_out, got, upd, last, prev, sems):
    sides = OWN // PIECES
    small = [(last_in, last, last_out), (prev_in, prev, prev_out)]

    def load(n):
        rows = pl.ds(n * sides, sides)
        return pltpu.make_async_copy(upd_in.at[:, rows], got.at[:, rows], sems.at[0, n])

    def store(n):
        rows = pl.ds(n * sides * 2 * ROUNDS, sides * 2 * ROUNDS)
        return pltpu.make_async_copy(upd.at[rows], upd_out.at[rows], sems.at[1, n])

    loads = [load(n) for n in range(PIECES)]
    stores = [store(n) for n in range(PIECES)]
    for n, (start, middle, end) in enumerate(small):
        loads.append(pltpu.make_async_copy(start, middle, sems.at[0, PIECES + n]))
        stores.append(pltpu.make_async_copy(middle, end, sems.at[1, PIECES + n]))
    for copy in loads:
        copy.start()
    for n, copy in enumerate(loads):
        copy.wait()
        if n < PIECES:
            for k in range(ROUNDS):
                block = got[k, n * sides : (n + 1) * sides, :]
                for part in range(2):
                    where = n * sides * 2 * ROUNDS + 2 * k + part
                    upd[pl.ds(where, sides, stride=2 * ROUNDS), :] = block[
                        :, part * 128 : part * 128 + 128
                    ]
        stores[n].start()
    for copy in stores:
        copy.wait()


def scratch():
    dma = pltpu.SemaphoreType.DMA
    return [
        pltpu.VMEM((2, ROUNDS, SHARE, BLOCK), BF16),
        pltpu.VMEM((ROUNDS, BLOCK, SIDES), BF16),
        pltpu.VMEM((WIDE, SHARE), F32),
        pltpu.VMEM((SHARE, ROWS * SHARE), BF16),
        pltpu.VMEM((BLOCK, COLS * BLOCK), BF16),
        pltpu.VMEM((256, SIDES), F32),
        pltpu.VMEM((2, COLS, WIDE, 256), BF16),
        pltpu.VMEM((2, COLS, WIDE, 256), BF16),
        pltpu.VMEM((ROWS, WIDE, SHARE), BF16),
        pltpu.VMEM((RING, WIDE, 2 * SHARE), BF16),
        pltpu.VMEM((ROWS, WIDE, 2 * SHARE), BF16),
        pltpu.VMEM((WIDE, 2 * SHARE), F32),
        pltpu.VMEM((2, WIDE, SHARE), F32),
        pltpu.VMEM((2, RING, WIDE, 2 * SHARE), BF16),
        pltpu.VMEM((SLOTS, RING * WIDE, BLOCK), F32),
        pltpu.VMEM((STEPS, 2, WIDE // 2, BLOCK), BF16),
        pltpu.VMEM((SLOTS, 2, WIDE // 2, BLOCK), BF16),
        pltpu.VMEM((STEPS, 2, WIDE, BLOCK), BF16),
        pltpu.VMEM((SLOTS, 2, WIDE, BLOCK), BF16),
        pltpu.VMEM((128, BLOCK), F32),
        pltpu.VMEM((ROUNDS, OWN, BLOCK), F32),
        pltpu.VMEM((ROUNDS, OWN, BLOCK), F32),
        pltpu.VMEM((OWN, BLOCK), BF16),
        pltpu.VMEM((OWN, BLOCK), F32),
        pltpu.VMEM((COLS, OWN, BLOCK), BF16),
        pltpu.VMEM((COLS, OWN, BLOCK), BF16),
        pltpu.VMEM((OWN, BLOCK), F32),
        dma((2, GROUPS + 1)),
        dma((GROUPS + 1,)),
        dma(()),
        dma(()),
        dma(()),
        dma((2,)),
        dma(()),
        dma((GROUPS + 1,)),
        dma(()),
        dma((2,)),
        dma((ROWS,)),
        dma((ROWS,)),
        dma((RING,)),
        dma((ROWS,)),
        dma(()),
        dma(()),
        dma(()),
        dma((2, RING)),
        dma(()),
        dma((SLOTS,)),
        dma(()),
        dma((SLOTS,)),
        dma((COLS,)),
        dma((COLS,)),
        dma(()),
    ]


def per_device(factor_panel, solved_prev, rhs_last, inv_last, inv_prev):
    panel = factor_panel.transpose(1, 2, 0, 3).reshape(ROUNDS, SHARE, BLOCK)
    known = solved_prev.reshape(ROUNDS, BLOCK, SIDES)
    anywhere = pl.BlockSpec(memory_space=pl.ANY)
    out_shape = [
        jax.ShapeDtypeStruct((OWN * ROUNDS * 2, 128), F32),
        jax.ShapeDtypeStruct((WIDE, SHARE), F32),
        jax.ShapeDtypeStruct((OWN, BLOCK), F32),
    ]
    results = pl.pallas_call(
        kernel,
        out_shape=[jax.ShapeDtypeStruct((ROUNDS, OWN, BLOCK), F32)] + out_shape[1:],
        in_specs=[anywhere] * 5,
        out_specs=[anywhere] * 3,
        scratch_shapes=scratch(),
        compiler_params=pltpu.CompilerParams(
            collective_id=0, has_side_effects=True, vmem_limit_bytes=60 * 1024 * 1024
        ),
        cost_estimate=pl.CostEstimate(
            flops=9 * 10**9, bytes_accessed=21 * 10**6, transcendentals=0
        ),
    )(panel, known, rhs_last.T, inv_last, inv_prev.reshape(BLOCK, COLS * BLOCK))
    updated, last_t, prev_t = pl.pallas_call(
        hand_over,
        out_shape=out_shape,
        in_specs=[anywhere] * 3,
        out_specs=[anywhere] * 3,
        scratch_shapes=[
            pltpu.VMEM((ROUNDS, OWN, BLOCK), F32),
            pltpu.VMEM((OWN * ROUNDS * 2 + 64, 128), F32),
            pltpu.VMEM((WIDE, SHARE), F32),
            pltpu.VMEM((OWN, BLOCK), F32),
        ]
        + [pltpu.SemaphoreType.DMA((2, PIECES + 2))],
        compiler_params=pltpu.CompilerParams(vmem_limit_bytes=60 * 1024 * 1024),
    )(*results)
    return updated.reshape(OWN, ROUNDS, 1, BLOCK), last_t.T, prev_t.T


def solution(mesh):
    in_specs = (
        P("row", None, "col", None),
        P(None, "col", None, None),
        P("row", "col"),
        P("row", None),
        P(None, "col", None, None),
    )
    out_specs = (P("row", None, "col", None), P("row", "col"), P("col", "row"))
    return jax.shard_map(
        per_device, mesh=mesh, in_specs=in_specs, out_specs=out_specs, check_vma=False
    )
```
